128 devices in a mesh: blk: 16 (over z, x), grp: 8 (over y, core).
Axes of the slice: x: 4, y: 4, z: 4, core: 2. Of those that a mesh axis runs over, the one named last changes fastest.
Arguments:
- right_side: float32 [256, 128, 256], P('blk', 'grp'), may hold values from -6 to 6
- weights: float32 [6, 256, 128, 256], P(None, 'blk', 'grp'), may hold values from 0.5 to 2
Outputs:
- solution_field: float32 [256, 128, 256], P('blk', 'grp')
- residual: float32 [256, 128, 256], P('blk', 'grp')
The draws below stay inside these ranges and needn't reach their ends.
All inputs are finite; a program needn't handle non-finite values.
Results may differ from the reference program's by a relative error of at most 0.0003.
Values sent between devices are 32-bit elements; how exact they have to be, the bound alone decides.
A program may use at most 128 MiB of HBM per device.

```python
import math
import jax
import jax.numpy as jnp
from jax import lax

LEVELS = 5
SWEEPS = 2
COARSE_SWEEPS = 8
CYCLES = 2
NX = 256
NY = 128
NZ = 256


def draw_right_side(key, part):
    key = jax.random.fold_in(key, 7)
    rough = jax.random.normal(key, (NX, NY, NZ), jnp.float32)
    return jnp.clip(rough, -6.0, 6.0)


def shard_levels(own_key, dims, shards, least, largest):
    factor_of, own = 1.0, jax.random.fold_in(own_key, 6)
    for axis_at, shards_of in shards:
        draws = jnp.exp(jax.random.uniform(jax.random.fold_in(own, axis_at), (shards_of,), jnp.float32, least / len(shards), largest / len(shards)))
        factor_of = factor_of * jnp.repeat(draws, dims[axis_at] // shards_of).reshape([-1 if axis == axis_at else 1 for axis in range(len(dims))])
    return factor_of


def setup_inputs(seed: int = 0) -> dict:
    arg_keys = jax.random.split(jax.random.key(seed), 3)
    right_side = draw_right_side(jax.random.fold_in(arg_keys[2], 71), 0)
    weights = jnp.clip(jnp.exp(math.log(2.0) - 1.3862944 * jax.random.uniform(arg_keys[1], (6, NX, NY, NZ), jnp.float32) ** shard_levels(arg_keys[1], (6, NX, NY, NZ), ((1, 16), (2, 8)), -0.2, 0.2)), 0.5, 2.0)
    return dict(right_side=right_side, weights=weights)


DIRECTIONS = ((0, 1), (0, -1), (1, 1), (1, -1), (2, 1), (2, -1))
relaxation = 0.7


def cut(array, along, begin, end):
    return lax.slice_in_dim(array, begin, end, axis=along)


def moved(array, along, sense):
    length = array.shape[along]
    zeros = jnp.zeros_like(cut(array, along, 0, 1))
    if sense == 1:
        return jnp.concatenate([zeros, cut(array, along, 0, length - 1)], axis=along)
    return jnp.concatenate([cut(array, along, 1, length), zeros], axis=along)


def restrict(array):
    shape = array.shape
    lead = shape[:-3]
    blocks = array.reshape(lead + (shape[-3] // 2, 2, shape[-2] // 2, 2, shape[-1] // 2, 2))
    return blocks.mean(axis=(-5, -3, -1))


def prolong(coarse):
    depth, height, width = coarse.shape
    wide = jnp.broadcast_to(coarse[:, None, :, None, :, None], (depth, 2, height, 2, width, 2))
    return wide.reshape(depth * 2, height * 2, width * 2)


def transposed(field, coeffs, centre):
    result = centre * field
    for index in range(6):
        along, sense = DIRECTIONS[index]
        result = result - moved(coeffs[index] * field, along, sense)
    return result


def sweep(field, source, coeffs, centre):
    return field + relaxation * (source - transposed(field, coeffs, centre)) / centre


def vcycle(level, source, coeffs_list, centres):
    coeffs = coeffs_list[level]
    centre = centres[level]
    field = relaxation * source / centre
    if level == LEVELS - 1:
        for count in range(COARSE_SWEEPS - 1):
            field = sweep(field, source, coeffs, centre)
        return field
    for count in range(SWEEPS - 1):
        field = sweep(field, source, coeffs, centre)
    coarse = restrict(source - transposed(field, coeffs, centre))
    field = field + prolong(vcycle(level + 1, coarse, coeffs_list, centres))
    for count in range(SWEEPS):
        field = sweep(field, source, coeffs, centre)
    return field


def reference(right_side, weights):
    coeffs_list = [weights]
    for level in range(LEVELS - 1):
        coeffs_list.append(restrict(coeffs_list[-1]) * 0.25)
    centres = [jnp.sum(coeffs, axis=0) for coeffs in coeffs_list]
    solution_field = vcycle(0, right_side, coeffs_list, centres)
    for count in range(CYCLES - 1):
        update = right_side - transposed(solution_field, coeffs_list[0], centres[0])
        solution_field = solution_field + vcycle(0, update, coeffs_list, centres)
    residual = right_side - transposed(solution_field, coeffs_list[0], centres[0])
    return solution_field, residual
```

```python
import functools

import jax
import jax.numpy as jnp
from jax import lax
from jax.experimental import pallas as pl
from jax.experimental.pallas import tpu as pltpu
from jax.sharding import PartitionSpec as P

MESH = pl.DeviceIdType.MESH
F32 = jnp.float32
BLK, GRP = 16, 8
OMEGA = 0.7
KEEP = 1.0 - OMEGA
NEIGHBOURS = tuple((dx, dy) for dx in (-1, 0, 1) for dy in (-1, 0, 1) if (dx, dy) != (0, 0))
CYCLES = 2


def lane_roll(v, n):
    return pltpu.roll(v, n % 128, v.ndim - 1)


def row_roll(v, n):
    axis = v.ndim - 2
    return pltpu.roll(v, n % v.shape[axis], axis)


def lane_index(shape):
    return lax.broadcasted_iota(jnp.int32, shape, len(shape) - 1)


def lane_swap(v, n):
    even = lax.rem(lax.div(lane_index(v.shape), n), 2) == 0
    return jnp.where(even, lane_roll(v, -n), lane_roll(v, n))


def split_dot(x, matrix):
    high = x.astype(jnp.bfloat16)
    rest = x - high.astype(F32)
    middle = rest.astype(jnp.bfloat16)
    low = (rest - middle.astype(F32)).astype(jnp.bfloat16)
    dot = functools.partial(jnp.dot, preferred_element_type=F32)
    return (dot(low, matrix) + dot(middle, matrix)) + dot(high, matrix)


def span(delta, size, halo, start):
    if delta == 1:
        return pl.ds(start + size - halo, halo), pl.ds(start - halo, halo)
    if delta == -1:
        return pl.ds(start, halo), pl.ds(start + size, halo)
    return pl.ds(start, size), pl.ds(start, size)


def kernel(
    rhs_ref, w_ref, sol_ref, res_ref,
    w0, f0, rc0, cr0, g0, big0, a0, b0, x0, s0,
    w1, f1, rc1, cr1, g1, big1, a1, b1, t1,
    w2, f2, rc2, cr2, g2, x2, big2, a2, b2, t2,
    w3row, w3, f3, rc3, cr3, g3row, g3, c3, t3,
    f4, rc4, tmp, dummy6, dummy1,
    send_sem, recv_sem, all_send, all_recv,
):
    b = lax.axis_index("blk")
    g = lax.axis_index("grp")

    def device(dx, dy):
        return (lax.rem(b + dx + BLK, BLK), lax.rem(g + dy + GRP, GRP))

    barrier = pltpu.get_barrier_semaphore()

    def greet(k, carry):
        pl.semaphore_signal(
            barrier, inc=1, device_id=device(lax.div(k, GRP), lax.rem(k, GRP)), device_id_type=MESH
        )
        return carry

    lax.fori_loop(1, BLK * GRP, greet, 0)

    def loop(begin, end, step):
        def one(index, carry):
            step(index)
            return carry

        lax.fori_loop(begin, end, one, 0)

    def copies(view, lead, size, halo, start_x, start_y, slot):
        out = []
        for n, (dx, dy) in enumerate(NEIGHBOURS):
            sx, tx = span(dx, size, halo, start_x)
            sy, ty = span(dy, size, halo, start_y)
            out.append(
                pltpu.make_async_remote_copy(
                    src_ref=view.at[lead + (sx, sy)],
                    dst_ref=view.at[lead + (tx, ty)],
                    send_sem=send_sem.at[slot, n],
                    recv_sem=recv_sem.at[slot, n],
                    device_id=device(dx, dy),
                    device_id_type=MESH,
                )
            )
        return out

    pending = []

    def start(batch):
        for copy in batch:
            copy.start()
        pending.extend(batch)

    def arrived(batch):
        for copy in batch:
            copy.wait_recv()

    def spread_all(row, gathered, slot):
        mine = pltpu.make_async_copy(row, gathered.at[:, b, pl.ds(g, 1), :], all_recv.at[slot])
        mine.start()

        def send(k, carry):
            pltpu.make_async_remote_copy(
                src_ref=row,
                dst_ref=gathered.at[:, b, pl.ds(g, 1), :],
                send_sem=all_send.at[slot],
                recv_sem=all_recv.at[slot],
                device_id=device(lax.div(k, GRP), lax.rem(k, GRP)),
                device_id_type=MESH,
            ).start()
            return carry

        lax.fori_loop(1, BLK * GRP, send, 0)

    def gathered_all(gathered, slot):
        pltpu.make_async_copy(gathered, gathered, all_recv.at[slot]).wait()

    def sent_all(dummy, slot):
        pltpu.make_async_copy(dummy, dummy, all_send.at[slot]).wait()

    def inside(rows, size, start_x, start_y):
        row = lax.broadcasted_iota(jnp.int32, (rows, 128), 0) + (g * size - start_y)

        def mask(plane):
            x = b * size + plane - start_x
            ok = jnp.logical_and(x >= 0, x < BLK * size)
            shifted = row + jnp.where(ok, 0, 1 << 20)
            return jnp.logical_and(shifted >= 0, shifted < GRP * size)

        return mask

    zi = lax.broadcasted_iota(jnp.int32, (256, 256), 0)
    ci = lax.broadcasted_iota(jnp.int32, (256, 256), 1)
    parted = jnp.where(ci < 128, 2 * ci, 2 * ci - 255)
    split = jnp.where(zi == parted, 1.0, 0.0).astype(jnp.bfloat16)
    parts = split_dot(rhs_ref[...].reshape(256, 256), split)
    g0[0, 0, 4:20, 4:20, :] = parts[:, :128].reshape(16, 16, 128)
    g0[0, 1, 4:20, 4:20, :] = parts[:, 128:].reshape(16, 16, 128)

    def part_weights(k):
        both = split_dot(w_ref[k].reshape(256, 256), split)
        w0[2 * k, 4:20, 4:20, :] = both[:, :128].reshape(16, 16, 128)
        w0[2 * k + 1, 4:20, 4:20, :] = both[:, 128:].reshape(16, 16, 128)

    loop(0, 6, part_weights)

    pl.semaphore_wait(barrier, BLK * GRP - 1)

    all_of = slice(None)
    w0_halo = copies(w0, (all_of,), 16, 3, 4, 4, 0)
    g0_halo = [copies(g0, (c, all_of), 16, 2, 4, 4, 3 + c) for c in range(CYCLES)]
    x0_halo = [copies(x0, (c, all_of), 16, 3, 4, 4, 5 + c) for c in range(CYCLES)]
    w1_halo = copies(w1, (all_of,), 8, 6, 6, 8, 1)
    g1_halo = [copies(g1, (c,), 8, 6, 6, 8, 7 + c) for c in range(CYCLES)]
    w2_halo = copies(w2, (all_of,), 4, 4, 4, 4, 2)
    x2_halo = [copies(x2, (c, all_of), 4, 4, 4, 4, 9 + c) for c in range(CYCLES)]

    start(g0_halo[0])
    start(w0_halo)

    def weights_1(i):
        for k in range(6):
            total = None
            for part in range(2):
                for dx in range(2):
                    for dy in range(2):
                        term = w0[2 * k + part, 4 + 2 * i + dx, pl.ds(4 + dy, 8, stride=2), :]
                        total = term if total is None else total + term
            w1[k, 6 + i, 8:16, :] = total * (1.0 / 32.0)

    loop(0, 8, weights_1)
    start(w1_halo)

    def weights_2(i):
        for k in range(6):
            total = None
            for dx in range(2):
                for dy in range(2):
                    term = w1[k, 6 + 2 * i + dx, pl.ds(8 + dy, 4, stride=2), :]
                    total = term if total is None else total + term
            w2[k, 4 + i, 4:8, :] = (total + lane_swap(total, 1)) * (1.0 / 32.0)

    loop(0, 4, weights_2)
    start(w2_halo)

    quad = lax.rem(lane_index((1, 128)), 4)

    def pack_quads(cells):
        out = cells[3]
        for n in range(3):
            out = jnp.where(quad == n, cells[n], out)
        return out

    def weights_3(k):
        cells = []
        for xl in range(2):
            for yl in range(2):
                total = None
                for dx in range(2):
                    for dy in range(2):
                        term = w2[k, 4 + 2 * xl + dx, pl.ds(4 + 2 * yl + dy, 1), :]
                        total = term if total is None else total + term
                cells.append((total + lane_swap(total, 2)) * (1.0 / 32.0))
        w3row[k] = pack_quads(cells)

    loop(0, 6, weights_3)
    spread_all(w3row, w3, 0)

    mask0 = inside(24, 16, 4, 4)
    mask1 = inside(24, 8, 6, 8)
    mask2 = inside(16, 4, 4, 4)
    lane24 = lane_index((24, 128))

    def relaxed(total, mask):
        return jnp.where(mask, OMEGA / total, 0.0)

    arrived(w0_halo)

    def fold_0(p):
        mask = mask0(p)
        rc = []
        for part in range(2):
            total = w0[part, p]
            for k in range(1, 6):
                total = total + w0[2 * k + part, p]
            rc.append(relaxed(total, mask))
            rc0[part, p] = rc[part]
            cr0[part, p] = total * (1.0 / OMEGA)
            f0[0 + part, p] = rc[part] * w0[0 + part, p - 1]
            f0[2 + part, p] = rc[part] * w0[2 + part, p + 1]
            f0[4 + part, p] = rc[part] * row_roll(w0[4 + part, p], 1)
            f0[6 + part, p] = rc[part] * row_roll(w0[6 + part, p], -1)
        f0[8, p] = rc[0] * jnp.where(lane24 == 0, 0.0, lane_roll(w0[9, p], 1))
        f0[9, p] = rc[1] * w0[8, p]
        f0[10, p] = rc[0] * w0[11, p]
        f0[11, p] = rc[1] * jnp.where(lane24 == 127, 0.0, lane_roll(w0[10, p], -1))

    loop(2, 22, fold_0)

    def sweep_0(u, p):
        e, o = u[0, p], u[1, p]
        out_e = KEEP * e + big0[0, p]
        out_o = KEEP * o + big0[1, p]
        out_e += f0[0, p] * u[0, p - 1]
        out_o += f0[1, p] * u[1, p - 1]
        out_e += f0[2, p] * u[0, p + 1]
        out_o += f0[3, p] * u[1, p + 1]
        out_e += f0[4, p] * row_roll(e, 1)
        out_o += f0[5, p] * row_roll(o, 1)
        out_e += f0[6, p] * row_roll(e, -1)
        out_o += f0[7, p] * row_roll(o, -1)
        out_e += f0[8, p] * lane_roll(o, 1)
        out_o += f0[9, p] * e
        out_e += f0[10, p] * o
        out_o += f0[11, p] * lane_roll(e, -1)
        return out_e, out_o

    def sweep_c(u, big, f, p, step):
        v = u[p]
        out = KEEP * v + big[p]
        out += f[0, p] * u[p - 1]
        out += f[1, p] * u[p + 1]
        out += f[2, p] * row_roll(v, 1)
        out += f[3, p] * row_roll(v, -1)
        out += f[4, p] * lane_roll(v, step)
        out += f[5, p] * lane_roll(v, -step)
        return out

    def fold_centre(w, rc, cr, p, mask):
        total = w[0, p]
        for k in range(1, 6):
            total = total + w[k, p]
        rc[p] = relaxed(total, mask)
        cr[p] = total * (1.0 / OMEGA)

    def fold_c(w, f, rc, p, step):
        r = rc[p]
        lanes = lane_index(r.shape)
        f[0, p] = r * w[0, p - 1]
        f[1, p] = r * w[1, p + 1]
        f[2, p] = r * row_roll(w[2, p], 1)
        f[3, p] = r * row_roll(w[3, p], -1)
        f[4, p] = r * jnp.where(lanes < step, 0.0, lane_roll(w[4, p], step))
        f[5, p] = r * jnp.where(lanes >= 128 - step, 0.0, lane_roll(w[5, p], -step))

    shape3 = (BLK, GRP, 128)

    def before(v):
        return jnp.concatenate([v[BLK - 1 :], v[: BLK - 1]], axis=0)

    def after(v):
        return jnp.concatenate([v[1:], v[:1]], axis=0)

    lane3 = lane_index(shape3)
    blk3 = lax.broadcasted_iota(jnp.int32, shape3, 0)
    grp3 = lax.broadcasted_iota(jnp.int32, shape3, 1)
    low_x = lax.rem(lax.div(lane3, 2), 2) == 0
    low_y = lax.rem(lane3, 2) == 0

    def shifts_3(v):
        r2, l2 = lane_roll(v, 2), lane_roll(v, -2)
        yield jnp.where(low_x, before(l2), r2)
        yield jnp.where(low_x, l2, after(r2))
        r1, l1 = lane_roll(v, 1), lane_roll(v, -1)
        yield jnp.where(low_y, row_roll(l1, 1), r1)
        yield jnp.where(low_y, l1, row_roll(r1, -1))
        yield lane_roll(v, 4)
        yield lane_roll(v, -4)

    def shifts_4(v):
        yield before(v)
        yield after(v)
        yield row_roll(v, 1)
        yield row_roll(v, -1)
        yield lane_roll(v, 8)
        yield lane_roll(v, -8)

    def octet(v):
        v = v + lane_swap(v, 1)
        v = v + lane_swap(v, 2)
        return v + lane_swap(v, 4)

    def fold_coarse():
        ws = [w3[k] for k in range(6)]
        total = ws[0] + ws[1] + ws[2] + ws[3] + ws[4] + ws[5]
        rc = OMEGA / total
        rc3[...] = rc
        cr3[...] = total * (1.0 / OMEGA)
        edge = (
            jnp.logical_and(blk3 == 0, low_x),
            jnp.logical_and(blk3 == BLK - 1, jnp.logical_not(low_x)),
            jnp.logical_and(grp3 == 0, low_y),
            jnp.logical_and(grp3 == GRP - 1, jnp.logical_not(low_y)),
            lane3 < 4,
            lane3 >= 124,
        )
        for k in range(6):
            moved = list(shifts_3(ws[k]))[k]
            f3[k] = jnp.where(edge[k], 0.0, rc * moved)
        total = None
        for k in range(6):
            coarse = octet(ws[k]) * (1.0 / 32.0)
            f4[k] = coarse
            total = coarse if total is None else total + coarse
        rc = OMEGA / total
        rc4[...] = rc
        edge = (blk3 == 0, blk3 == BLK - 1, grp3 == 0, grp3 == GRP - 1, lane3 < 8, lane3 >= 120)
        for k in range(6):
            moved = list(shifts_4(f4[k]))[k]
            f4[k] = jnp.where(edge[k], 0.0, rc * moved)

    def sweep_3(v, big):
        out = KEEP * v + big
        for k, moved in enumerate(shifts_3(v)):
            out += f3[k] * moved
        return out

    def sweep_4(v, big):
        out = KEEP * v + big
        for k, moved in enumerate(shifts_4(v)):
            out += f4[k] * moved
        return out

    def coarse_levels(source):
        big = rc3[...] * source
        u = sweep_3(big, big)
        left = (sweep_3(u, big) - u) * cr3[...]
        big_4 = rc4[...] * (octet(left) * 0.125)
        v = lax.fori_loop(0, 7, lambda n, v: sweep_4(v, big_4), big_4)
        u = u + v
        u = sweep_3(u, big)
        return sweep_3(u, big)

    for c in range(CYCLES):
        arrived(g0_halo[c])

        def source_0(p):
            for part in range(2):
                big0[part, p] = rc0[part, p] * g0[c, part, p]

        loop(2, 22, source_0)

        def down_0(p):
            a0[0, p], a0[1, p] = sweep_0(big0, p)

        loop(3, 21, down_0)

        def restrict_0(i):
            total = None
            for dx in range(2):
                p = 4 + 2 * i + dx
                e, o = sweep_0(a0, p)
                left = (e - a0[0, p]) * cr0[0, p] + (o - a0[1, p]) * cr0[1, p]
                total = left if total is None else total + left
            tmp[i] = total
            rows = tmp[i, pl.ds(4, 8, stride=2), :] + tmp[i, pl.ds(5, 8, stride=2), :]
            g1[c, 6 + i, 8:16, :] = rows * 0.125

        loop(0, 8, restrict_0)
        start(g1_halo[c])

        def keep_0(p):
            for part in range(2):
                x0[c, part, p, 4:20, :] = a0[part, p, 4:20, :]

        loop(4, 20, keep_0)
        start(x0_halo[c])

        if c == 0:
            arrived(w1_halo)
            loop(0, 20, lambda p: fold_centre(w1, rc1, cr1, p, mask1(p)))
            loop(1, 19, lambda p: fold_c(w1, f1, rc1, p, 1))
            arrived(w2_halo)
            loop(0, 12, lambda p: fold_centre(w2, rc2, cr2, p, mask2(p)))
            loop(1, 11, lambda p: fold_c(w2, f2, rc2, p, 2))
            gathered_all(w3, 0)
            fold_coarse()
        arrived(g1_halo[c])

        def source_1(p):
            big1[p] = rc1[p] * g1[c, p]

        loop(0, 20, source_1)

        def down_1(p):
            a1[p] = sweep_c(big1, big1, f1, p, 1)

        loop(1, 19, down_1)

        def restrict_1(i):
            total = None
            for dx in range(2):
                p = 2 + 2 * i + dx
                left = (sweep_c(a1, big1, f1, p, 1) - a1[p]) * cr1[p]
                total = left if total is None else total + left
            tmp[i] = total
            rows = tmp[i, pl.ds(4, 8, stride=2), :] + tmp[i, pl.ds(5, 8, stride=2), :]
            g2[2 + i, 2:10, :] = (rows + lane_swap(rows, 1)) * 0.125

        loop(0, 8, restrict_1)

        def source_2(p):
            big2[p] = rc2[p] * g2[p]

        loop(2, 10, source_2)

        def down_2(p):
            a2[p] = sweep_c(big2, big2, f2, p, 2)

        loop(3, 9, down_2)
        sums = []
        for xl in range(2):
            total = None
            for dx in range(2):
                p = 4 + 2 * xl + dx
                left = (sweep_c(a2, big2, f2, p, 2) - a2[p]) * cr2[p]
                total = left if total is None else total + left
            tmp[xl, 0:16, :] = (total + lane_swap(total, 2)) * 0.125
        cells = []
        for xl in range(2):
            for yl in range(2):
                cells.append(tmp[xl, pl.ds(4 + 2 * yl, 1), :] + tmp[xl, pl.ds(5 + 2 * yl, 1), :])
        g3row[c, 0] = pack_quads(cells)
        spread_all(g3row.at[c], g3.at[c], 1 + c)

        def keep_2(p):
            x2[c, 0, p, 4:8, :] = g2[p, 4:8, :]
            x2[c, 1, p, 4:8, :] = a2[p, 4:8, :]

        loop(4, 8, keep_2)
        start(x2_halo[c])

        gathered_all(g3.at[c], 1 + c)
        c3[1:17] = coarse_levels(g3[c, 0])

        quad8 = lax.rem(lane_index((8, 128)), 4)

        def widen_3(q):
            v = c3[b + lax.div(q, 2)]
            xl = lax.rem(q, 2)
            for yl in range(2):
                own = jnp.where(quad8 == 2 * xl + yl, v, 0.0)
                out = own
                pair = own + lane_swap(own, 1)
                out = pair + lane_swap(pair, 2)
                for dy in range(2):
                    t3[q, pl.ds(8 + 2 * yl + dy, 8, stride=4), :] = out

        loop(0, 6, widen_3)
        arrived(x2_halo[c])

        def correct_2(p):
            big2[p] = rc2[p] * x2[c, 0, p]
            add = t3[lax.div(p, 2), pl.ds(4 + 4 * g, 16), :]
            b2[p] = jnp.where(mask2(p), x2[c, 1, p] + add, 0.0)

        loop(0, 12, correct_2)

        def up_2a(p):
            a2[p] = sweep_c(b2, big2, f2, p, 2)

        loop(1, 11, up_2a)

        def up_2b(i):
            t2[i] = sweep_c(a2, big2, f2, i + 2, 2)
            rows = t2[i, 2:10, :]
            t1[i, pl.ds(4, 8, stride=2), :] = rows
            t1[i, pl.ds(5, 8, stride=2), :] = rows

        loop(0, 8, up_2b)

        def correct_1(p):
            b1[p] = jnp.where(mask1(p), a1[p] + t1[lax.div(p - 2, 2)], 0.0)

        loop(2, 18, correct_1)

        def up_1a(p):
            a1[p] = sweep_c(b1, big1, f1, p, 1)

        loop(3, 17, up_1a)

        def up_1b(i):
            tmp[i] = sweep_c(a1, big1, f1, i + 4, 1)
            rows = tmp[i, 6:18, :]
            s0[i, pl.ds(0, 12, stride=2), :] = rows
            s0[i, pl.ds(1, 12, stride=2), :] = rows

        loop(0, 12, up_1b)

        arrived(x0_halo[c])

        def correct_0(p):
            add = s0[lax.div(p, 2)]
            mask = mask0(p)
            for part in range(2):
                b0[part, p] = jnp.where(mask, x0[c, part, p] + add, 0.0)

        loop(1, 23, correct_0)

        def up_0a(p):
            a0[0, p], a0[1, p] = sweep_0(b0, p)

        loop(2, 22, up_0a)

        def up_0b(p):
            b0[0, p], b0[1, p] = sweep_0(a0, p)

        loop(3, 21, up_0b)

        if c + 1 < CYCLES:

            def update(p):
                parts = sweep_0(b0, p)
                for part in range(2):
                    left = (parts[part] - b0[part, p]) * cr0[part, p]
                    g0[c + 1, part, p, 4:20, :] = left[4:20]
                    sol_ref[p - 4, :, 128 * part : 128 * part + 128] = b0[part, p, 4:20, :]

            loop(4, 20, update)
            start(g0_halo[c + 1])

    def finish(p):
        parts = sweep_0(b0, p)
        lefts = [(parts[part] - b0[part, p]) * cr0[part, p] for part in range(2)]
        for part in range(2):
            res_ref[p - 4, :, 128 * part : 128 * part + 128] = lefts[part][4:20]
            sol_ref[p - 4, :, 128 * part : 128 * part + 128] += b0[part, p, 4:20, :]

    loop(4, 20, finish)
    zi = lax.broadcasted_iota(jnp.int32, (256, 256), 1)
    ci = lax.broadcasted_iota(jnp.int32, (256, 256), 0)
    parted = jnp.where(ci < 128, 2 * ci, 2 * ci - 255)
    joined = jnp.where(zi == parted, 1.0, 0.0).astype(jnp.bfloat16)
    for ref in (sol_ref, res_ref):
        ref[...] = split_dot(ref[...].reshape(256, 256), joined).reshape(16, 16, 256)

    for copy in pending:
        copy.wait_send()
    sent_all(dummy6, 0)
    for c in range(CYCLES):
        sent_all(dummy1, 1 + c)


def body(right_side, weights):
    vmem = pl.BlockSpec(memory_space=pltpu.VMEM)
    field = jax.ShapeDtypeStruct((16, 16, 256), F32)
    f0 = (24, 24, 128)
    f1 = (20, 24, 128)
    f2 = (12, 16, 128)
    f3 = (BLK, GRP, 128)

    def buf(*shape):
        return pltpu.VMEM(shape, F32)

    return pl.pallas_call(
        kernel,
        out_shape=(field, field),
        in_specs=[vmem, vmem],
        out_specs=(vmem, vmem),
        scratch_shapes=[
            buf(12, *f0), buf(12, *f0), buf(2, *f0), buf(2, *f0), buf(2, 2, *f0), buf(2, *f0),
            buf(2, *f0), buf(2, *f0), buf(2, 2, *f0), buf(12, 24, 128),
            buf(6, *f1), buf(6, *f1), buf(*f1), buf(*f1), buf(2, *f1), buf(*f1), buf(*f1), buf(*f1), buf(8, 24, 128),
            buf(6, *f2), buf(6, *f2), buf(*f2), buf(*f2), buf(*f2), buf(2, 2, *f2), buf(*f2), buf(*f2), buf(*f2),
            buf(8, 16, 128),
            buf(6, 1, 128), buf(6, *f3), buf(6, *f3), buf(*f3), buf(*f3), buf(2, 1, 1, 128), buf(2, 1, *f3),
            buf(18, 8, 128), buf(6, 48, 128),
            buf(6, *f3), buf(*f3), buf(12, 24, 128), buf(127, 6, 1, 128), buf(127, 1, 1, 128),
            pltpu.SemaphoreType.DMA((11, 8)),
            pltpu.SemaphoreType.DMA((11, 8)),
            pltpu.SemaphoreType.DMA((3,)),
            pltpu.SemaphoreType.DMA((3,)),
        ],
        compiler_params=pltpu.CompilerParams(
            collective_id=0, has_side_effects=True, vmem_limit_bytes=56 * 1024 * 1024
        ),
    )(right_side, weights)


def solution(mesh):
    return jax.shard_map(
        body,
        mesh=mesh,
        in_specs=(P("blk", "grp", None), P(None, "blk", "grp", None)),
        out_specs=(P("blk", "grp", None), P("blk", "grp", None)),
        check_vma=False,
    )
```

```python
import functools

import jax
import jax.numpy as jnp
from jax import lax
from jax.experimental import pallas as pl
from jax.experimental.pallas import tpu as pltpu
from jax.sharding import PartitionSpec as P

MESH = pl.DeviceIdType.MESH
F32 = jnp.float32
BLK, GRP = 16, 8
OMEGA = 0.7
KEEP = 1.0 - OMEGA
NEIGHBOURS = tuple((dx, dy) for dx in (-1, 0, 1) for dy in (-1, 0, 1) if (dx, dy) != (0, 0))
CYCLES = 2


def lane_roll(v, n):
    return pltpu.roll(v, n % 128, v.ndim - 1)


def row_roll(v, n):
    axis = v.ndim - 2
    return pltpu.roll(v, n % v.shape[axis], axis)


def lane_index(shape):
    return lax.broadcasted_iota(jnp.int32, shape, len(shape) - 1)


def lane_swap(v, n):
    even = (lane_index(v.shape[-2:]) & n) == 0
    even = jnp.broadcast_to(even, v.shape)
    return jnp.where(even, lane_roll(v, -n), lane_roll(v, n))


def split_dot(x, matrix):
    high = x.astype(jnp.bfloat16)
    rest = x - high.astype(F32)
    middle = rest.astype(jnp.bfloat16)
    low = (rest - middle.astype(F32)).astype(jnp.bfloat16)
    dot = functools.partial(jnp.dot, preferred_element_type=F32)
    return (dot(low, matrix) + dot(middle, matrix)) + dot(high, matrix)


def span(delta, size, halo, start):
    if delta == 1:
        return pl.ds(start + size - halo, halo), pl.ds(start - halo, halo)
    if delta == -1:
        return pl.ds(start, halo), pl.ds(start + size, halo)
    return pl.ds(start, size), pl.ds(start, size)


def kernel(
    rhs_ref, w_ref, sol_ref, res_ref,
    w0, f0, rc0, cr0, g0, big0, a0, b0, x0, s0,
    w1, f1, rc1, cr1, g1, big1, a1, b1, t1,
    w2, f2, rc2, cr2, g2, x2, big2, a2, b2, t2,
    w3row, w3, f3, rc3, cr3, g3row, g3, c3, t3,
    f4, rc4, tmp, dummy6, dummy1,
    send_sem, recv_sem, all_send, all_recv,
):
    b = lax.axis_index("blk")
    g = lax.axis_index("grp")

    def device(dx, dy):
        return (lax.rem(b + dx + BLK, BLK), lax.rem(g + dy + GRP, GRP))

    barrier = pltpu.get_barrier_semaphore()

    def greet(k, carry):
        pl.semaphore_signal(
            barrier, inc=1, device_id=device(lax.div(k, GRP), lax.rem(k, GRP)), device_id_type=MESH
        )
        return carry

    lax.fori_loop(1, BLK * GRP, greet, 0)

    def loop(begin, end, step):
        def one(index, carry):
            step(index)
            return carry

        lax.fori_loop(begin, end, one, 0)

    def copies(view, lead, size, halo, start_x, start_y, slot):
        out = []
        for n, (dx, dy) in enumerate(NEIGHBOURS):
            sx, tx = span(dx, size, halo, start_x)
            sy, ty = span(dy, size, halo, start_y)
            out.append(
                pltpu.make_async_remote_copy(
                    src_ref=view.at[lead + (sx, sy)],
                    dst_ref=view.at[lead + (tx, ty)],
                    send_sem=send_sem.at[slot, n],
                    recv_sem=recv_sem.at[slot, n],
                    device_id=device(dx, dy),
                    device_id_type=MESH,
                )
            )
        return out

    pending = []

    def start(batch):
        for copy in batch:
            copy.start()
        pending.extend(batch)

    def arrived(batch):
        for copy in batch:
            copy.wait_recv()

    def spread_all(row, gathered, slot):
        mine = pltpu.make_async_copy(row, gathered.at[:, b, pl.ds(g, 1), :], all_recv.at[slot])
        mine.start()

        def send(k, carry):
            pltpu.make_async_remote_copy(
                src_ref=row,
                dst_ref=gathered.at[:, b, pl.ds(g, 1), :],
                send_sem=all_send.at[slot],
                recv_sem=all_recv.at[slot],
                device_id=device(lax.div(k, GRP), lax.rem(k, GRP)),
                device_id_type=MESH,
            ).start()
            return carry

        lax.fori_loop(1, BLK * GRP, send, 0)

    def gathered_all(gathered, slot):
        pltpu.make_async_copy(gathered, gathered, all_recv.at[slot]).wait()

    def sent_all(dummy, slot):
        pltpu.make_async_copy(dummy, dummy, all_send.at[slot]).wait()

    def inside(rows, size, start_x, start_y):
        def mask(p, n):
            shape = (n, rows, 128)
            x = lax.broadcasted_iota(jnp.int32, shape, 0) + (b * size + p - start_x)
            y = lax.broadcasted_iota(jnp.int32, shape, 1) + (g * size - start_y)
            ok_x = jnp.logical_and(x >= 0, x < BLK * size)
            ok_y = jnp.logical_and(y >= 0, y < GRP * size)
            return jnp.logical_and(ok_x, ok_y)

        return mask

    def planes(begin, end, size, step):
        count = (end - begin) // size
        if count == 1:
            step(begin, size)
        elif count > 1:
            loop(0, count, lambda i: step(begin + i * size, size))
        if end - begin > count * size:
            step(begin + count * size, end - begin - count * size)

    def pairs(v):
        both = v.reshape((v.shape[0] // 2, 2) + v.shape[1:])
        return both[:, 0] + both[:, 1]

    def doubled(v):
        wide = jnp.broadcast_to(v[:, None], (v.shape[0], 2) + v.shape[1:])
        return wide.reshape((2 * v.shape[0],) + v.shape[1:])

    zi = lax.broadcasted_iota(jnp.int32, (256, 256), 0)
    ci = lax.broadcasted_iota(jnp.int32, (256, 256), 1)
    parted = jnp.where(ci < 128, 2 * ci, 2 * ci - 255)
    split = jnp.where(zi == parted, 1.0, 0.0).astype(jnp.bfloat16)
    parts = split_dot(rhs_ref[...].reshape(256, 256), split)
    g0[0, 0, 4:20, 4:20, :] = parts[:, :128].reshape(16, 16, 128)
    g0[0, 1, 4:20, 4:20, :] = parts[:, 128:].reshape(16, 16, 128)

    def part_weights(k):
        both = split_dot(w_ref[k].reshape(256, 256), split)
        w0[2 * k, 4:20, 4:20, :] = both[:, :128].reshape(16, 16, 128)
        w0[2 * k + 1, 4:20, 4:20, :] = both[:, 128:].reshape(16, 16, 128)

    loop(0, 6, part_weights)

    pl.semaphore_wait(barrier, BLK * GRP - 1)

    all_of = slice(None)
    w0_halo = copies(w0, (all_of,), 16, 3, 4, 4, 0)
    g0_halo = [copies(g0, (c, all_of), 16, 2, 4, 4, 3 + c) for c in range(CYCLES)]
    x0_halo = [copies(x0, (c, all_of), 16, 3, 4, 4, 5 + c) for c in range(CYCLES)]
    w1_halo = copies(w1, (all_of,), 8, 6, 6, 8, 1)
    g1_halo = [copies(g1, (c,), 8, 6, 6, 8, 7 + c) for c in range(CYCLES)]
    w2_halo = copies(w2, (all_of,), 4, 4, 4, 4, 2)
    x2_halo = [copies(x2, (c, all_of), 4, 4, 4, 4, 9 + c) for c in range(CYCLES)]

    start(g0_halo[0])
    start(w0_halo)

    def weights_1(k):
        total = None
        for part in range(2):
            for dy in range(2):
                term = pairs(w0[2 * k + part, 4:20, pl.ds(4 + dy, 8, stride=2), :])
                total = term if total is None else total + term
        w1[k, 6:14, 8:16, :] = total * (1.0 / 32.0)

    loop(0, 6, weights_1)
    start(w1_halo)
    for k in range(6):
        total = None
        for dy in range(2):
            term = pairs(w1[k, 6:14, pl.ds(8 + dy, 4, stride=2), :])
            total = term if total is None else total + term
        w2[k, 4:8, 4:8, :] = (total + lane_swap(total, 1)) * (1.0 / 32.0)
    start(w2_halo)

    quad = lane_index((1, 128)) & 3

    def pack_quads(cells):
        out = cells[3]
        for n in range(3):
            out = jnp.where(quad == n, cells[n], out)
        return out

    for k in range(6):
        total = pairs(w2[k, 4:8, 4:8, :])
        total = (total + lane_swap(total, 2)) * (1.0 / 32.0)
        cells = []
        for xl in range(2):
            for yl in range(2):
                cells.append(total[xl, 2 * yl : 2 * yl + 1] + total[xl, 2 * yl + 1 : 2 * yl + 2])
        w3row[k] = pack_quads(cells)
    spread_all(w3row, w3, 0)

    mask0 = inside(24, 16, 4, 4)
    mask1 = inside(24, 8, 6, 8)
    mask2 = inside(16, 4, 4, 4)

    def relaxed(total, mask):
        return jnp.where(mask, OMEGA / total, 0.0)

    arrived(w0_halo)

    def fold_0(p, n):
        here, low, high = pl.ds(p, n), pl.ds(p - 1, n), pl.ds(p + 1, n)
        mask = mask0(p, n)
        lanes = lane_index((n, 24, 128))
        rc = []
        for part in range(2):
            total = w0[part, here]
            for k in range(1, 6):
                total = total + w0[2 * k + part, here]
            rc.append(relaxed(total, mask))
            rc0[part, here] = rc[part]
            cr0[part, here] = total * (1.0 / OMEGA)
            f0[0 + part, here] = rc[part] * w0[0 + part, low]
            f0[2 + part, here] = rc[part] * w0[2 + part, high]
            f0[4 + part, here] = rc[part] * row_roll(w0[4 + part, here], 1)
            f0[6 + part, here] = rc[part] * row_roll(w0[6 + part, here], -1)
        f0[8, here] = rc[0] * jnp.where(lanes == 0, 0.0, lane_roll(w0[9, here], 1))
        f0[9, here] = rc[1] * w0[8, here]
        f0[10, here] = rc[0] * w0[11, here]
        f0[11, here] = rc[1] * jnp.where(lanes == 127, 0.0, lane_roll(w0[10, here], -1))

    planes(2, 22, 5, fold_0)

    def sweep_0(u, p, n):
        here, low, high = pl.ds(p, n), pl.ds(p - 1, n), pl.ds(p + 1, n)
        e, o = u[0, here], u[1, here]
        out_e = KEEP * e + big0[0, here]
        out_o = KEEP * o + big0[1, here]
        out_e += f0[0, here] * u[0, low]
        out_o += f0[1, here] * u[1, low]
        out_e += f0[2, here] * u[0, high]
        out_o += f0[3, here] * u[1, high]
        out_e += f0[4, here] * row_roll(e, 1)
        out_o += f0[5, here] * row_roll(o, 1)
        out_e += f0[6, here] * row_roll(e, -1)
        out_o += f0[7, here] * row_roll(o, -1)
        out_e += f0[8, here] * lane_roll(o, 1)
        out_o += f0[9, here] * e
        out_e += f0[10, here] * o
        out_o += f0[11, here] * lane_roll(e, -1)
        return out_e, out_o

    def sweep_c(u, big, f, p, n, step):
        here = pl.ds(p, n)
        v = u[here]
        out = KEEP * v + big[here]
        out += f[0, here] * u[pl.ds(p - 1, n)]
        out += f[1, here] * u[pl.ds(p + 1, n)]
        out += f[2, here] * row_roll(v, 1)
        out += f[3, here] * row_roll(v, -1)
        out += f[4, here] * lane_roll(v, step)
        out += f[5, here] * lane_roll(v, -step)
        return out

    def fold_centre(w, rc, cr, p, n, mask):
        here = pl.ds(p, n)
        total = w[0, here]
        for k in range(1, 6):
            total = total + w[k, here]
        rc[here] = relaxed(total, mask)
        cr[here] = total * (1.0 / OMEGA)

    def fold_c(w, f, rc, p, n, step):
        here = pl.ds(p, n)
        r = rc[here]
        lanes = lane_index(r.shape)
        f[0, here] = r * w[0, pl.ds(p - 1, n)]
        f[1, here] = r * w[1, pl.ds(p + 1, n)]
        f[2, here] = r * row_roll(w[2, here], 1)
        f[3, here] = r * row_roll(w[3, here], -1)
        f[4, here] = r * jnp.where(lanes < step, 0.0, lane_roll(w[4, here], step))
        f[5, here] = r * jnp.where(lanes >= 128 - step, 0.0, lane_roll(w[5, here], -step))

    shape3 = (BLK, GRP, 128)

    def before(v):
        return jnp.concatenate([v[BLK - 1 :], v[: BLK - 1]], axis=0)

    def after(v):
        return jnp.concatenate([v[1:], v[:1]], axis=0)

    lane3 = lane_index(shape3)
    blk3 = lax.broadcasted_iota(jnp.int32, shape3, 0)
    grp3 = lax.broadcasted_iota(jnp.int32, shape3, 1)
    low_x = (lane3 & 2) == 0
    low_y = (lane3 & 1) == 0

    def shifts_3(v):
        r2, l2 = lane_roll(v, 2), lane_roll(v, -2)
        yield jnp.where(low_x, before(l2), r2)
        yield jnp.where(low_x, l2, after(r2))
        r1, l1 = lane_roll(v, 1), lane_roll(v, -1)
        yield jnp.where(low_y, row_roll(l1, 1), r1)
        yield jnp.where(low_y, l1, row_roll(r1, -1))
        yield lane_roll(v, 4)
        yield lane_roll(v, -4)

    def shifts_4(v):
        yield before(v)
        yield after(v)
        yield row_roll(v, 1)
        yield row_roll(v, -1)
        yield lane_roll(v, 8)
        yield lane_roll(v, -8)

    def octet(v):
        v = v + lane_swap(v, 1)
        v = v + lane_swap(v, 2)
        return v + lane_swap(v, 4)

    def fold_coarse():
        ws = [w3[k] for k in range(6)]
        total = ws[0] + ws[1] + ws[2] + ws[3] + ws[4] + ws[5]
        rc = OMEGA / total
        rc3[...] = rc
        cr3[...] = total * (1.0 / OMEGA)
        edge = (
            jnp.logical_and(blk3 == 0, low_x),
            jnp.logical_and(blk3 == BLK - 1, jnp.logical_not(low_x)),
            jnp.logical_and(grp3 == 0, low_y),
            jnp.logical_and(grp3 == GRP - 1, jnp.logical_not(low_y)),
            lane3 < 4,
            lane3 >= 124,
        )
        for k in range(6):
            moved = list(shifts_3(ws[k]))[k]
            f3[k] = jnp.where(edge[k], 0.0, rc * moved)
        total = None
        for k in range(6):
            coarse = octet(ws[k]) * (1.0 / 32.0)
            f4[k] = coarse
            total = coarse if total is None else total + coarse
        rc = OMEGA / total
        rc4[...] = rc
        edge = (blk3 == 0, blk3 == BLK - 1, grp3 == 0, grp3 == GRP - 1, lane3 < 8, lane3 >= 120)
        for k in range(6):
            moved = list(shifts_4(f4[k]))[k]
            f4[k] = jnp.where(edge[k], 0.0, rc * moved)

    def sweep_3(v, big):
        out = KEEP * v + big
        for k, moved in enumerate(shifts_3(v)):
            out += f3[k] * moved
        return out

    def sweep_4(v, big):
        out = KEEP * v + big
        for k, moved in enumerate(shifts_4(v)):
            out += f4[k] * moved
        return out

    def coarse_levels(source):
        big = rc3[...] * source
        u = sweep_3(big, big)
        left = (sweep_3(u, big) - u) * cr3[...]
        big_4 = rc4[...] * (octet(left) * 0.125)
        v = lax.fori_loop(0, 7, lambda n, v: sweep_4(v, big_4), big_4)
        u = u + v
        u = sweep_3(u, big)
        return sweep_3(u, big)

    for c in range(CYCLES):
        arrived(g0_halo[c])

        def source_0(p, n):
            here = pl.ds(p, n)
            for part in range(2):
                big0[part, here] = rc0[part, here] * g0[c, part, here]

        planes(2, 22, 10, source_0)

        def down_0(p, n):
            here = pl.ds(p, n)
            a0[0, here], a0[1, here] = sweep_0(big0, p, n)

        planes(3, 21, 9, down_0)

        def restrict_0(p, n):
            here = pl.ds(p, n)
            e, o = sweep_0(a0, p, n)
            left = (e - a0[0, here]) * cr0[0, here] + (o - a0[1, here]) * cr0[1, here]
            m = n // 2
            tmp[0:m] = pairs(left)
            rows = tmp[0:m, pl.ds(4, 8, stride=2), :] + tmp[0:m, pl.ds(5, 8, stride=2), :]
            g1[c, pl.ds(lax.div(p, 2) + 4, m), 8:16, :] = rows * 0.125

        planes(4, 20, 8, restrict_0)
        start(g1_halo[c])
        for part in range(2):
            x0[c, part, 4:20, 4:20, :] = a0[part, 4:20, 4:20, :]
        start(x0_halo[c])

        if c == 0:
            arrived(w1_halo)
            planes(0, 20, 10, lambda p, n: fold_centre(w1, rc1, cr1, p, n, mask1(p, n)))
            planes(1, 19, 6, lambda p, n: fold_c(w1, f1, rc1, p, n, 1))
            arrived(w2_halo)
            planes(0, 12, 12, lambda p, n: fold_centre(w2, rc2, cr2, p, n, mask2(p, n)))
            planes(1, 11, 10, lambda p, n: fold_c(w2, f2, rc2, p, n, 2))
            gathered_all(w3, 0)
            fold_coarse()
        arrived(g1_halo[c])
        big1[...] = rc1[...] * g1[c]
        a1[1:19] = sweep_c(big1, big1, f1, 1, 18, 1)
        left = (sweep_c(a1, big1, f1, 2, 16, 1) - a1[2:18]) * cr1[2:18]
        tmp[0:8] = pairs(left)
        rows = tmp[0:8, pl.ds(4, 8, stride=2), :] + tmp[0:8, pl.ds(5, 8, stride=2), :]
        g2[2:10, 2:10, :] = (rows + lane_swap(rows, 1)) * 0.125
        big2[2:10] = rc2[2:10] * g2[2:10]
        a2[3:9] = sweep_c(big2, big2, f2, 3, 6, 2)
        left = (sweep_c(a2, big2, f2, 4, 4, 2) - a2[4:8]) * cr2[4:8]
        left = pairs(left)
        tmp[0:2, 0:16, :] = (left + lane_swap(left, 2)) * 0.125
        cells = []
        for xl in range(2):
            for yl in range(2):
                cells.append(tmp[xl, pl.ds(4 + 2 * yl, 1), :] + tmp[xl, pl.ds(5 + 2 * yl, 1), :])
        g3row[c, 0] = pack_quads(cells)
        spread_all(g3row.at[c], g3.at[c], 1 + c)
        x2[c, 0, 4:8, 4:8, :] = g2[4:8, 4:8, :]
        x2[c, 1, 4:8, 4:8, :] = a2[4:8, 4:8, :]
        start(x2_halo[c])
        gathered_all(g3.at[c], 1 + c)
        c3[1:17] = coarse_levels(g3[c, 0])

        near = c3[pl.ds(b, 3)]
        quads = lane_index((3, 8, 128)) & 3
        for xl in range(2):
            for yl in range(2):
                own = jnp.where(quads == 2 * xl + yl, near, 0.0)
                own = own + lane_swap(own, 1)
                own = own + lane_swap(own, 2)
                for dy in range(2):
                    t3[:, xl, pl.ds(8 + 2 * yl + dy, 8, stride=4), :] = own
        arrived(x2_halo[c])
        big2[...] = rc2[...] * x2[c, 0]
        add = doubled(t3[:, :, pl.ds(4 + 4 * g, 16), :].reshape(6, 16, 128))
        b2[...] = jnp.where(mask2(0, 12), x2[c, 1] + add, 0.0)
        a2[1:11] = sweep_c(b2, big2, f2, 1, 10, 2)
        t2[...] = sweep_c(a2, big2, f2, 2, 8, 2)
        rows = t2[:, 2:10, :]
        t1[:, pl.ds(4, 8, stride=2), :] = rows
        t1[:, pl.ds(5, 8, stride=2), :] = rows

        b1[2:18] = jnp.where(mask1(2, 16), a1[2:18] + doubled(t1[...]), 0.0)
        a1[3:17] = sweep_c(b1, big1, f1, 3, 14, 1)
        tmp[...] = sweep_c(a1, big1, f1, 4, 12, 1)
        rows = tmp[:, 6:18, :]
        s0[:, pl.ds(0, 12, stride=2), :] = rows
        s0[:, pl.ds(1, 12, stride=2), :] = rows

        arrived(x0_halo[c])

        def correct_0(p, n):
            here = pl.ds(p, n)
            add = doubled(s0[pl.ds(lax.div(p, 2), n // 2)])
            mask = mask0(p, n)
            for part in range(2):
                b0[part, here] = jnp.where(mask, x0[c, part, here] + add, 0.0)

        planes(0, 24, 8, correct_0)

        def up_0a(p, n):
            here = pl.ds(p, n)
            a0[0, here], a0[1, here] = sweep_0(b0, p, n)

        planes(2, 22, 10, up_0a)

        def up_0b(p, n):
            here = pl.ds(p, n)
            b0[0, here], b0[1, here] = sweep_0(a0, p, n)

        planes(3, 21, 9, up_0b)

        def update(p, n):
            here, out = pl.ds(p, n), pl.ds(p - 4, n)
            swept = sweep_0(b0, p, n)
            for part in range(2):
                lanes = pl.ds(128 * part, 128)
                u = b0[part, here]
                left = ((swept[part] - u) * cr0[part, here])[:, 4:20, :]
                if c + 1 < CYCLES:
                    g0[c + 1, part, here, 4:20, :] = left
                else:
                    res_ref[out, :, lanes] = left
                u = u[:, 4:20, :]
                sol_ref[out, :, lanes] = u if c == 0 else sol_ref[out, :, lanes] + u

        planes(4, 20, 8, update)
        if c + 1 < CYCLES:
            start(g0_halo[c + 1])

    zi = lax.broadcasted_iota(jnp.int32, (256, 256), 1)
    ci = lax.broadcasted_iota(jnp.int32, (256, 256), 0)
    parted = jnp.where(ci < 128, 2 * ci, 2 * ci - 255)
    joined = jnp.where(zi == parted, 1.0, 0.0).astype(jnp.bfloat16)
    for ref in (sol_ref, res_ref):
        ref[...] = split_dot(ref[...].reshape(256, 256), joined).reshape(16, 16, 256)

    for copy in pending:
        copy.wait_send()
    sent_all(dummy6, 0)
    for c in range(CYCLES):
        sent_all(dummy1, 1 + c)


def body(right_side, weights):
    vmem = pl.BlockSpec(memory_space=pltpu.VMEM)
    field = jax.ShapeDtypeStruct((16, 16, 256), F32)
    f0 = (24, 24, 128)
    f1 = (20, 24, 128)
    f2 = (12, 16, 128)
    f3 = (BLK, GRP, 128)

    def buf(*shape):
        return pltpu.VMEM(shape, F32)

    return pl.pallas_call(
        kernel,
        out_shape=(field, field),
        in_specs=[vmem, vmem],
        out_specs=(vmem, vmem),
        scratch_shapes=[
            buf(12, *f0), buf(12, *f0), buf(2, *f0), buf(2, *f0), buf(2, 2, *f0), buf(2, *f0),
            buf(2, *f0), buf(2, *f0), buf(2, 2, *f0), buf(12, 24, 128),
            buf(6, *f1), buf(6, *f1), buf(*f1), buf(*f1), buf(2, *f1), buf(*f1), buf(*f1), buf(*f1), buf(8, 24, 128),
            buf(6, *f2), buf(6, *f2), buf(*f2), buf(*f2), buf(*f2), buf(2, 2, *f2), buf(*f2), buf(*f2), buf(*f2),
            buf(8, 16, 128),
            buf(6, 1, 128), buf(6, *f3), buf(6, *f3), buf(*f3), buf(*f3), buf(2, 1, 1, 128), buf(2, 1, *f3),
            buf(18, 8, 128), buf(3, 2, 48, 128),
            buf(6, *f3), buf(*f3), buf(12, 24, 128), buf(127, 6, 1, 128), buf(127, 1, 1, 128),
            pltpu.SemaphoreType.DMA((11, 8)),
            pltpu.SemaphoreType.DMA((11, 8)),
            pltpu.SemaphoreType.DMA((3,)),
            pltpu.SemaphoreType.DMA((3,)),
        ],
        compiler_params=pltpu.CompilerParams(
            collective_id=0, has_side_effects=True, vmem_limit_bytes=56 * 1024 * 1024
        ),
    )(right_side, weights)


def solution(mesh):
    return jax.shard_map(
        body,
        mesh=mesh,
        in_specs=(P("blk", "grp", None), P(None, "blk", "grp", None)),
        out_specs=(P("blk", "grp", None), P("blk", "grp", None)),
        check_vma=False,
    )
```

```python
import functools

import jax
import jax.numpy as jnp
from jax import lax
from jax.experimental import pallas as pl
from jax.experimental.pallas import tpu as pltpu
from jax.sharding import PartitionSpec as P

MESH = pl.DeviceIdType.MESH
F32 = jnp.float32
BLK, GRP = 16, 8
OMEGA = 0.7
KEEP = 1.0 - OMEGA
FACES = ((1, 0), (-1, 0), (0, 1), (0, -1))
CORNERS = ((1, 1), (1, -1), (-1, 1), (-1, -1))


def distance(offset):
    dx, dy = offset
    x, y, z = dx % 4, dy // 2, dx // 4
    return min(x, 4 - x) + min(y, 4 - y) + min(z, 4 - z)


EVERYONE = sorted(((dx, dy) for dx in range(BLK) for dy in range(GRP) if dx or dy), key=distance, reverse=True)
CYCLES = 2


def lane_roll(v, n):
    return pltpu.roll(v, n % 128, v.ndim - 1)


def row_roll(v, n):
    axis = v.ndim - 2
    return pltpu.roll(v, n % v.shape[axis], axis)


def lane_index(shape):
    return lax.broadcasted_iota(jnp.int32, shape, len(shape) - 1)


def lane_swap(v, n):
    even = (lane_index(v.shape[-2:]) & n) == 0
    even = jnp.broadcast_to(even, v.shape)
    return jnp.where(even, lane_roll(v, -n), lane_roll(v, n))


def split_dot(x, matrix):
    high = x.astype(jnp.bfloat16)
    rest = x - high.astype(F32)
    middle = rest.astype(jnp.bfloat16)
    low = (rest - middle.astype(F32)).astype(jnp.bfloat16)
    dot = functools.partial(jnp.dot, preferred_element_type=F32)
    return (dot(low, matrix) + dot(middle, matrix)) + dot(high, matrix)


def piece(delta, size, start, first, count):
    if delta == 1:
        return pl.ds(start + size + 1 - first - count, count), pl.ds(start + 1 - first - count, count)
    if delta == -1:
        return pl.ds(start + first - 1, count), pl.ds(start + size + first - 1, count)
    return pl.ds(start, size), pl.ds(start, size)


def kernel(
    rhs_ref, w_ref, sol_ref, res_ref,
    raw, w0, f0, cr0, g0, big0, a0, b0, x0, s0,
    w1, f1, rc1, cr1, g1, big1, a1, b1, t1,
    w2, f2, rc2, cr2, g2, x2, big2, a2, b2, t2,
    w3, f3, rc3, cr3, g3row, g3, c3, t3,
    f4, rc4, tmp, dummy, dummy1,
    load_sem, send_sem, recv_sem, all_send, all_recv,
):
    b = lax.axis_index("blk")
    g = lax.axis_index("grp")

    loads = [pltpu.make_async_copy(w_ref.at[k], raw.at[k], load_sem.at[k]) for k in range(6)]
    loads.append(pltpu.make_async_copy(rhs_ref, raw.at[6], load_sem.at[6]))
    for copy in loads:
        copy.start()

    def device(dx, dy):
        return (lax.rem(b + dx + BLK, BLK), lax.rem(g + dy + GRP, GRP))

    barrier = pltpu.get_barrier_semaphore()

    def greet(k, carry):
        pl.semaphore_signal(
            barrier, inc=1, device_id=device(lax.div(k, GRP), lax.rem(k, GRP)), device_id_type=MESH
        )
        return carry

    lax.fori_loop(1, BLK * GRP, greet, 0)

    def loop(begin, end, step):
        def one(index, carry):
            step(index)
            return carry

        lax.fori_loop(begin, end, one, 0)

    def patch(view, lead, fields, level, dx, dy, layers_x, layers_y):
        size, start_x, start_y = level
        sx, tx = piece(dx, size, start_x, *layers_x)
        sy, ty = piece(dy, size, start_y, *layers_y)
        rows = fields * (layers_x[1] if dx else size) * (layers_y[1] if dy else size)
        return view.at[lead + (sx, sy)], view.at[lead + (tx, ty)], device(dx, dy), rows

    def faces(view, lead, fields, level, layers):
        return [
            patch(view, lead, fields, level, dx, dy, (1, layers), (1, layers)) for dx, dy in FACES
        ]

    def corners(view, lead, fields, level, layers_x, layers_y):
        return [patch(view, lead, fields, level, dx, dy, layers_x, layers_y) for dx, dy in CORNERS]

    def inward(view, each, level, layer):
        return [
            patch(view, (pl.ds(k * each, each),), each, level, dx, dy, (layer, 1), (layer, 1))
            for k, (dx, dy) in enumerate(FACES)
        ]

    batches = []

    def batch(parts):
        index = len(batches)
        copies = [
            pltpu.make_async_remote_copy(
                src_ref=src,
                dst_ref=dst,
                send_sem=send_sem.at[index],
                recv_sem=recv_sem.at[index],
                device_id=to,
                device_id_type=MESH,
            )
            for src, dst, to, _ in parts
        ]
        rows = sum(part[3] for part in parts)
        batches.append((copies, dummy.at[pl.ds(0, rows)], index))
        return batches[-1]

    def start(one):
        for copy in one[0]:
            copy.start()

    def arrived(one):
        pltpu.make_async_copy(one[1], one[1], recv_sem.at[one[2]]).wait()

    def departed(one):
        pltpu.make_async_copy(one[1], one[1], send_sem.at[one[2]]).wait()

    def spread(src, dst, offsets, slot):
        for dx, dy in offsets:
            pltpu.make_async_remote_copy(
                src_ref=src,
                dst_ref=dst,
                send_sem=all_send.at[slot],
                recv_sem=all_recv.at[slot],
                device_id=device(dx, dy),
                device_id_type=MESH,
            ).start()

    def spread_all(c):
        row, mine = g3row.at[c], g3.at[c, b, pl.ds(g, 1), :]
        pltpu.make_async_copy(row, mine, all_recv.at[2 + c]).start()
        spread(row, mine, EVERYONE, 2 + c)

    def wait_for(ref, sem):
        pltpu.make_async_copy(ref, ref, sem).wait()

    def inside(rows, size, start_x, start_y):
        def mask(p, n):
            shape = (n, rows, 128)
            x = lax.broadcasted_iota(jnp.int32, shape, 0) + (b * size + p - start_x)
            y = lax.broadcasted_iota(jnp.int32, shape, 1) + (g * size - start_y)
            ok_x = jnp.logical_and(x >= 0, x < BLK * size)
            ok_y = jnp.logical_and(y >= 0, y < GRP * size)
            return jnp.logical_and(ok_x, ok_y)

        return mask

    def planes(begin, end, size, step):
        count = (end - begin) // size
        if count == 1:
            step(begin, size)
        elif count > 1:
            loop(0, count, lambda i: step(begin + i * size, size))
        if end - begin > count * size:
            step(begin + count * size, end - begin - count * size)

    def pairs(v):
        both = v.reshape((v.shape[0] // 2, 2) + v.shape[1:])
        return both[:, 0] + both[:, 1]

    def doubled(v):
        wide = jnp.broadcast_to(v[:, None], (v.shape[0], 2) + v.shape[1:])
        return wide.reshape((2 * v.shape[0],) + v.shape[1:])

    zi = lax.broadcasted_iota(jnp.int32, (256, 256), 0)
    ci = lax.broadcasted_iota(jnp.int32, (256, 256), 1)
    parted = jnp.where(ci < 128, 2 * ci, 2 * ci - 255)
    split = jnp.where(zi == parted, 1.0, 0.0).astype(jnp.bfloat16)

    def part_weights(k):
        pltpu.make_async_copy(w_ref.at[k], raw.at[k], load_sem.at[k]).wait()
        both = split_dot(raw[k].reshape(256, 256), split)
        w0[2 * k, 4:20, 4:20, :] = both[:, :128].reshape(16, 16, 128)
        w0[2 * k + 1, 4:20, 4:20, :] = both[:, 128:].reshape(16, 16, 128)

    loop(0, 6, part_weights)
    loads[6].wait()
    both = split_dot(raw[6].reshape(256, 256), split)
    for part in range(2):
        total = w0[part, 4:20, 4:20, :]
        for k in range(1, 6):
            total = total + w0[2 * k + part, 4:20, 4:20, :]
        source = both[:, 128 * part : 128 * part + 128].reshape(16, 16, 128)
        g0[0, part, 4:20, 4:20, :] = (OMEGA / total) * source

    pl.semaphore_wait(barrier, BLK * GRP - 1)

    every = slice(None)
    level_0, level_1, level_2 = (16, 4, 4), (8, 6, 8), (4, 4, 4)

    def halo(view, lead, fields, level, layers, corner):
        return faces(view, lead, fields, level, layers) + corners(
            view, lead, fields, level, (1, corner), (1, corner)
        )

    cycles = range(CYCLES)
    g0_halo = [batch(halo(g0, (c, every), 2, level_0, 2, 1)) for c in cycles]
    g1_halo = [batch(halo(g1, (c,), 1, level_1, 6, 5)) for c in cycles]
    x0_halo = [batch(halo(x0, (c, every), 2, level_0, 3, 2)) for c in cycles]
    x2_halo = [batch(halo(x2, (c, every), 2, level_2, 4, 4)) for c in cycles]
    w0_halo = batch(halo(w0, (every,), 12, level_0, 2, 2) + inward(w0, 2, level_0, 3))
    w1_halo = batch(
        halo(w1, (every,), 6, level_1, 5, 3)
        + inward(w1, 1, level_1, 6)
        + corners(w1, (every,), 6, level_1, (4, 2), (1, 2))
        + corners(w1, (every,), 6, level_1, (1, 2), (4, 2))
    )
    w2_halo = batch(halo(w2, (every,), 6, level_2, 3, 4) + inward(w2, 1, level_2, 4))

    start(g0_halo[0])
    start(w0_halo)

    def weights_1(k):
        total = None
        for part in range(2):
            for dy in range(2):
                term = pairs(w0[2 * k + part, 4:20, pl.ds(4 + dy, 8, stride=2), :])
                total = term if total is None else total + term
        w1[k, 6:14, 8:16, :] = total * (1.0 / 32.0)

    loop(0, 6, weights_1)
    start(w1_halo)
    total = w1[0, 6:14, 8:16, :]
    for k in range(1, 6):
        total = total + w1[k, 6:14, 8:16, :]
    rc1[...] = OMEGA / total
    for k in range(6):
        total = None
        for dy in range(2):
            term = pairs(w1[k, 6:14, pl.ds(8 + dy, 4, stride=2), :])
            total = term if total is None else total + term
        w2[k, 4:8, 4:8, :] = (total + lane_swap(total, 1)) * (1.0 / 32.0)

    quad = lane_index((1, 128)) & 3

    def pack_quads(cells):
        out = cells[3]
        for n in range(3):
            out = jnp.where(quad == n, cells[n], out)
        return out

    for k in range(6):
        total = pairs(w2[k, 4:8, 4:8, :])
        total = (total + lane_swap(total, 2)) * (1.0 / 32.0)
        cells = []
        for xl in range(2):
            for yl in range(2):
                cells.append(total[xl, 2 * yl : 2 * yl + 1] + total[xl, 2 * yl + 1 : 2 * yl + 2])
        w3[k, b, pl.ds(g, 1), :] = pack_quads(cells)
    mine = w3.at[:, b, pl.ds(g, 1), :]
    spread(mine, mine, [(0, dy) for dy in range(1, GRP)], 0)

    mask0 = inside(24, 16, 4, 4)
    mask1 = inside(24, 8, 6, 8)
    mask2 = inside(16, 4, 4, 4)

    def relaxed(total, mask):
        return jnp.where(mask, OMEGA / total, 0.0)

    arrived(w0_halo)

    def fold_0(p, n):
        here, low, high = pl.ds(p, n), pl.ds(p - 1, n), pl.ds(p + 1, n)
        mask = mask0(p, n)
        lanes = lane_index((n, 24, 128))
        rc = []
        for part in range(2):
            total = w0[part, here]
            for k in range(1, 6):
                total = total + w0[2 * k + part, here]
            rc.append(relaxed(total, mask))
            cr0[part, here] = total * (1.0 / OMEGA)
            f0[0 + part, here] = rc[part] * w0[0 + part, low]
            f0[2 + part, here] = rc[part] * w0[2 + part, high]
            f0[4 + part, here] = rc[part] * row_roll(w0[4 + part, here], 1)
            f0[6 + part, here] = rc[part] * row_roll(w0[6 + part, here], -1)
        f0[8, here] = rc[0] * jnp.where(lanes == 0, 0.0, lane_roll(w0[9, here], 1))
        f0[9, here] = rc[1] * w0[8, here]
        f0[10, here] = rc[0] * w0[11, here]
        f0[11, here] = rc[1] * jnp.where(lanes == 127, 0.0, lane_roll(w0[10, here], -1))

    planes(2, 22, 5, fold_0)

    def sweep_0(u, p, n):
        here, low, high = pl.ds(p, n), pl.ds(p - 1, n), pl.ds(p + 1, n)
        e, o = u[0, here], u[1, here]
        out_e = KEEP * e + big0[0, here]
        out_o = KEEP * o + big0[1, here]
        out_e += f0[0, here] * u[0, low]
        out_o += f0[1, here] * u[1, low]
        out_e += f0[2, here] * u[0, high]
        out_o += f0[3, here] * u[1, high]
        out_e += f0[4, here] * row_roll(e, 1)
        out_o += f0[5, here] * row_roll(o, 1)
        out_e += f0[6, here] * row_roll(e, -1)
        out_o += f0[7, here] * row_roll(o, -1)
        out_e += f0[8, here] * lane_roll(o, 1)
        out_o += f0[9, here] * e
        out_e += f0[10, here] * o
        out_o += f0[11, here] * lane_roll(e, -1)
        return out_e, out_o

    def sweep_c(u, big, f, p, n, step):
        here = pl.ds(p, n)
        v = u[here]
        out = KEEP * v + big[here]
        out += f[0, here] * u[pl.ds(p - 1, n)]
        out += f[1, here] * u[pl.ds(p + 1, n)]
        out += f[2, here] * row_roll(v, 1)
        out += f[3, here] * row_roll(v, -1)
        out += f[4, here] * lane_roll(v, step)
        out += f[5, here] * lane_roll(v, -step)
        return out

    def fold_c(w, f, cr, p, n, step, mask):
        here = pl.ds(p, n)
        total = w[0, here]
        for k in range(1, 6):
            total = total + w[k, here]
        r = relaxed(total, mask)
        cr[here] = total * (1.0 / OMEGA)
        lanes = lane_index(r.shape)
        f[0, here] = r * w[0, pl.ds(p - 1, n)]
        f[1, here] = r * w[1, pl.ds(p + 1, n)]
        f[2, here] = r * row_roll(w[2, here], 1)
        f[3, here] = r * row_roll(w[3, here], -1)
        f[4, here] = r * jnp.where(lanes < step, 0.0, lane_roll(w[4, here], step))
        f[5, here] = r * jnp.where(lanes >= 128 - step, 0.0, lane_roll(w[5, here], -step))
        return r

    shape3 = (BLK, GRP, 128)

    def before(v):
        return jnp.concatenate([v[BLK - 1 :], v[: BLK - 1]], axis=0)

    def after(v):
        return jnp.concatenate([v[1:], v[:1]], axis=0)

    lane3 = lane_index(shape3)
    blk3 = lax.broadcasted_iota(jnp.int32, shape3, 0)
    grp3 = lax.broadcasted_iota(jnp.int32, shape3, 1)
    low_x = (lane3 & 2) == 0
    low_y = (lane3 & 1) == 0

    def shifts_3(v):
        r2, l2 = lane_roll(v, 2), lane_roll(v, -2)
        yield jnp.where(low_x, before(l2), r2)
        yield jnp.where(low_x, l2, after(r2))
        r1, l1 = lane_roll(v, 1), lane_roll(v, -1)
        yield jnp.where(low_y, row_roll(l1, 1), r1)
        yield jnp.where(low_y, l1, row_roll(r1, -1))
        yield lane_roll(v, 4)
        yield lane_roll(v, -4)

    def shifts_4(v):
        yield before(v)
        yield after(v)
        yield row_roll(v, 1)
        yield row_roll(v, -1)
        yield lane_roll(v, 8)
        yield lane_roll(v, -8)

    def octet(v):
        v = v + lane_swap(v, 1)
        v = v + lane_swap(v, 2)
        return v + lane_swap(v, 4)

    def fold_coarse():
        ws = [w3[k] for k in range(6)]
        total = ws[0] + ws[1] + ws[2] + ws[3] + ws[4] + ws[5]
        rc = OMEGA / total
        rc3[...] = rc
        cr3[...] = total * (1.0 / OMEGA)
        edge = (
            jnp.logical_and(blk3 == 0, low_x),
            jnp.logical_and(blk3 == BLK - 1, jnp.logical_not(low_x)),
            jnp.logical_and(grp3 == 0, low_y),
            jnp.logical_and(grp3 == GRP - 1, jnp.logical_not(low_y)),
            lane3 < 4,
            lane3 >= 124,
        )
        for k in range(6):
            moved = list(shifts_3(ws[k]))[k]
            f3[k] = jnp.where(edge[k], 0.0, rc * moved)
        total = None
        for k in range(6):
            coarse = octet(ws[k]) * (1.0 / 32.0)
            f4[k] = coarse
            total = coarse if total is None else total + coarse
        rc = OMEGA / total
        rc4[...] = rc
        edge = (blk3 == 0, blk3 == BLK - 1, grp3 == 0, grp3 == GRP - 1, lane3 < 8, lane3 >= 120)
        for k in range(6):
            moved = list(shifts_4(f4[k]))[k]
            f4[k] = jnp.where(edge[k], 0.0, rc * moved)

    def sweep_3(v, big):
        out = KEEP * v + big
        for k, moved in enumerate(shifts_3(v)):
            out += f3[k] * moved
        return out

    def sweep_4(v, big):
        out = KEEP * v + big
        for k, moved in enumerate(shifts_4(v)):
            out += f4[k] * moved
        return out

    def coarse_levels(source):
        big = rc3[...] * source
        u = sweep_3(big, big)
        left = (sweep_3(u, big) - u) * cr3[...]
        big_4 = rc4[...] * (octet(left) * 0.125)
        v = lax.fori_loop(0, 7, lambda n, v: sweep_4(v, big_4), big_4)
        u = u + v
        u = sweep_3(u, big)
        return sweep_3(u, big)

    for c in range(CYCLES):
        arrived(g0_halo[c])

        def source_0(p, n):
            here = pl.ds(p, n)
            mask = mask0(p, n)
            for part in range(2):
                big0[part, here] = jnp.where(mask, g0[c, part, here], 0.0)

        planes(2, 22, 10, source_0)

        def down_0(p, n):
            here = pl.ds(p, n)
            a0[0, here], a0[1, here] = sweep_0(big0, p, n)

        planes(3, 21, 9, down_0)

        def restrict_0(p, n):
            here = pl.ds(p, n)
            e, o = sweep_0(a0, p, n)
            left = (e - a0[0, here]) * cr0[0, here] + (o - a0[1, here]) * cr0[1, here]
            m = n // 2
            tmp[0:m] = pairs(left)
            rows = tmp[0:m, pl.ds(4, 8, stride=2), :] + tmp[0:m, pl.ds(5, 8, stride=2), :]
            here = pl.ds(lax.div(p, 2) - 2, m)
            there = pl.ds(lax.div(p, 2) + 4, m)
            g1[c, there, 8:16, :] = rc1[here] * (rows * 0.125)

        planes(4, 20, 8, restrict_0)
        start(g1_halo[c])
        for part in range(2):
            x0[c, part, 4:20, 4:20, :] = a0[part, 4:20, 4:20, :]
        start(x0_halo[c])

        if c == 0:
            start(w2_halo)
            wait_for(w3.at[:, pl.ds(0, GRP - 1), pl.ds(0, 1), :], all_recv.at[0])
            block = w3.at[:, b]
            spread(block, block, [(dx, 0) for dx in range(1, BLK)], 1)
            arrived(w1_halo)
            planes(1, 19, 6, lambda p, n: fold_c(w1, f1, cr1, p, n, 1, mask1(p, n)))
        arrived(g1_halo[c])
        big1[...] = jnp.where(mask1(0, 20), g1[c], 0.0)
        a1[1:19] = sweep_c(big1, big1, f1, 1, 18, 1)
        left = (sweep_c(a1, big1, f1, 2, 16, 1) - a1[2:18]) * cr1[2:18]
        tmp[0:8] = pairs(left)
        rows = tmp[0:8, pl.ds(4, 8, stride=2), :] + tmp[0:8, pl.ds(5, 8, stride=2), :]
        g2[2:10, 2:10, :] = (rows + lane_swap(rows, 1)) * 0.125
        if c == 0:
            arrived(w2_halo)
            rc2[1:11] = fold_c(w2, f2, cr2, 1, 10, 2, mask2(1, 10))
        big2[2:10] = rc2[2:10] * g2[2:10]
        a2[3:9] = sweep_c(big2, big2, f2, 3, 6, 2)
        left = (sweep_c(a2, big2, f2, 4, 4, 2) - a2[4:8]) * cr2[4:8]
        left = pairs(left)
        tmp[0:2, 0:16, :] = (left + lane_swap(left, 2)) * 0.125
        cells = []
        for xl in range(2):
            for yl in range(2):
                cells.append(tmp[xl, pl.ds(4 + 2 * yl, 1), :] + tmp[xl, pl.ds(5 + 2 * yl, 1), :])
        g3row[c] = pack_quads(cells)
        spread_all(c)
        x2[c, 0, 4:8, 4:8, :] = big2[4:8, 4:8, :]
        x2[c, 1, 4:8, 4:8, :] = a2[4:8, 4:8, :]
        start(x2_halo[c])
        if c == 0:
            wait_for(w3.at[:, pl.ds(0, BLK - 1)], all_recv.at[1])
            fold_coarse()
        wait_for(g3.at[c], all_recv.at[2 + c])
        c3[1:17] = coarse_levels(g3[c])

        near = c3[pl.ds(b, 3)]
        quads = lane_index((3, 8, 128)) & 3
        for xl in range(2):
            for yl in range(2):
                own = jnp.where(quads == 2 * xl + yl, near, 0.0)
                own = own + lane_swap(own, 1)
                own = own + lane_swap(own, 2)
                for dy in range(2):
                    t3[:, xl, pl.ds(8 + 2 * yl + dy, 8, stride=4), :] = own
        arrived(x2_halo[c])
        inside_2 = mask2(0, 12)
        big2[...] = jnp.where(inside_2, x2[c, 0], 0.0)
        add = doubled(t3[:, :, pl.ds(4 + 4 * g, 16), :].reshape(6, 16, 128))
        b2[...] = jnp.where(inside_2, x2[c, 1] + add, 0.0)
        a2[1:11] = sweep_c(b2, big2, f2, 1, 10, 2)
        t2[...] = sweep_c(a2, big2, f2, 2, 8, 2)
        rows = t2[:, 2:10, :]
        t1[:, pl.ds(4, 8, stride=2), :] = rows
        t1[:, pl.ds(5, 8, stride=2), :] = rows

        b1[2:18] = jnp.where(mask1(2, 16), a1[2:18] + doubled(t1[...]), 0.0)
        a1[3:17] = sweep_c(b1, big1, f1, 3, 14, 1)
        tmp[...] = sweep_c(a1, big1, f1, 4, 12, 1)
        rows = tmp[:, 6:18, :]
        s0[:, pl.ds(0, 12, stride=2), :] = rows
        s0[:, pl.ds(1, 12, stride=2), :] = rows

        arrived(x0_halo[c])

        def correct_0(p, n):
            here = pl.ds(p, n)
            add = doubled(s0[pl.ds(lax.div(p, 2), n // 2)])
            mask = mask0(p, n)
            for part in range(2):
                b0[part, here] = jnp.where(mask, x0[c, part, here] + add, 0.0)

        planes(0, 24, 8, correct_0)

        def up_0a(p, n):
            here = pl.ds(p, n)
            a0[0, here], a0[1, here] = sweep_0(b0, p, n)

        planes(2, 22, 10, up_0a)

        def up_0b(p, n):
            here = pl.ds(p, n)
            b0[0, here], b0[1, here] = sweep_0(a0, p, n)

        planes(3, 21, 9, up_0b)

        def update(p, n):
            here, out = pl.ds(p, n), pl.ds(p - 4, n)
            swept = sweep_0(b0, p, n)
            for part in range(2):
                lanes = pl.ds(128 * part, 128)
                u = b0[part, here]
                change = swept[part] - u
                if c + 1 < CYCLES:
                    g0[c + 1, part, here, 4:20, :] = change[:, 4:20, :]
                else:
                    res_ref[out, :, lanes] = (change * cr0[part, here])[:, 4:20, :]
                u = u[:, 4:20, :]
                sol_ref[out, :, lanes] = u if c == 0 else sol_ref[out, :, lanes] + u

        planes(4, 20, 8, update)
        if c + 1 < CYCLES:
            start(g0_halo[c + 1])

    zi = lax.broadcasted_iota(jnp.int32, (256, 256), 1)
    ci = lax.broadcasted_iota(jnp.int32, (256, 256), 0)
    parted = jnp.where(ci < 128, 2 * ci, 2 * ci - 255)
    joined = jnp.where(zi == parted, 1.0, 0.0).astype(jnp.bfloat16)
    for ref in (sol_ref, res_ref):
        ref[...] = split_dot(ref[...].reshape(256, 256), joined).reshape(16, 16, 256)

    for one in batches:
        departed(one)
    wait_for(w3.at[:, pl.ds(0, GRP - 1), pl.ds(0, 1), :], all_send.at[0])
    wait_for(w3.at[:, pl.ds(0, BLK - 1)], all_send.at[1])
    for c in cycles:
        wait_for(dummy1, all_send.at[2 + c])


def body(right_side, weights):
    vmem = pl.BlockSpec(memory_space=pltpu.VMEM)
    field = jax.ShapeDtypeStruct((16, 16, 256), F32)
    f0 = (24, 24, 128)
    f1 = (20, 24, 128)
    f2 = (12, 16, 128)
    f3 = (BLK, GRP, 128)

    def buf(*shape):
        return pltpu.VMEM(shape, F32)

    return pl.pallas_call(
        kernel,
        out_shape=(field, field),
        in_specs=[pl.BlockSpec(memory_space=pl.ANY)] * 2,
        out_specs=(vmem, vmem),
        scratch_shapes=[
            buf(7, 16, 16, 256),
            buf(12, *f0), buf(12, *f0), buf(2, *f0), buf(2, 2, *f0), buf(2, *f0),
            buf(2, *f0), buf(2, *f0), buf(2, 2, *f0), buf(12, 24, 128),
            buf(6, *f1), buf(6, *f1), buf(8, 8, 128), buf(*f1), buf(2, *f1), buf(*f1), buf(*f1), buf(*f1), buf(8, 24, 128),
            buf(6, *f2), buf(6, *f2), buf(*f2), buf(*f2), buf(*f2), buf(2, 2, *f2), buf(*f2), buf(*f2), buf(*f2),
            buf(8, 16, 128),
            buf(6, *f3), buf(6, *f3), buf(*f3), buf(*f3), buf(2, 1, 128), buf(2, *f3),
            buf(18, 8, 128), buf(3, 2, 48, 128),
            buf(6, *f3), buf(*f3), buf(12, 24, 128), buf(2048, 128), buf(127, 1, 128),
            pltpu.SemaphoreType.DMA((7,)),
            pltpu.SemaphoreType.DMA((11,)),
            pltpu.SemaphoreType.DMA((11,)),
            pltpu.SemaphoreType.DMA((4,)),
            pltpu.SemaphoreType.DMA((4,)),
        ],
        compiler_params=pltpu.CompilerParams(
            collective_id=0, has_side_effects=True, vmem_limit_bytes=56 * 1024 * 1024
        ),
    )(right_side, weights)


def solution(mesh):
    return jax.shard_map(
        body,
        mesh=mesh,
        in_specs=(P("blk", "grp", None), P(None, "blk", "grp", None)),
        out_specs=(P("blk", "grp", None), P("blk", "grp", None)),
        check_vma=False,
    )
```

```python
import functools

import jax
import jax.numpy as jnp
from jax import lax
from jax.experimental import pallas as pl
from jax.experimental.pallas import tpu as pltpu
from jax.sharding import PartitionSpec as P

MESH = pl.DeviceIdType.MESH
F32 = jnp.float32
BLK, GRP = 16, 8
OMEGA = 0.7
KEEP = 1.0 - OMEGA
FACES = ((1, 0), (-1, 0), (0, 1), (0, -1))
CORNERS = ((1, 1), (1, -1), (-1, 1), (-1, -1))


def distance(offset):
    dx, dy = offset
    x, y, z = dx % 4, dy // 2, dx // 4
    return min(x, 4 - x) + min(y, 4 - y) + min(z, 4 - z)


EVERYONE = sorted(((dx, dy) for dx in range(BLK) for dy in range(GRP) if dx or dy), key=distance, reverse=True)
CYCLES = 2


def lane_roll(v, n):
    return pltpu.roll(v, n % 128, v.ndim - 1)


def row_roll(v, n):
    axis = v.ndim - 2
    return pltpu.roll(v, n % v.shape[axis], axis)


def lane_index(shape):
    return lax.broadcasted_iota(jnp.int32, shape, len(shape) - 1)


def lane_swap(v, n):
    even = (lane_index(v.shape[-2:]) & n) == 0
    even = jnp.broadcast_to(even, v.shape)
    return jnp.where(even, lane_roll(v, -n), lane_roll(v, n))


def split_dot(x, matrix):
    high = x.astype(jnp.bfloat16)
    rest = x - high.astype(F32)
    middle = rest.astype(jnp.bfloat16)
    low = (rest - middle.astype(F32)).astype(jnp.bfloat16)
    dot = functools.partial(jnp.dot, preferred_element_type=F32)
    return (dot(low, matrix) + dot(middle, matrix)) + dot(high, matrix)


def piece(delta, size, start, first, count):
    if delta == 1:
        return pl.ds(start + size + 1 - first - count, count), pl.ds(start + 1 - first - count, count)
    if delta == -1:
        return pl.ds(start + first - 1, count), pl.ds(start + size + first - 1, count)
    return pl.ds(start, size), pl.ds(start, size)


def kernel(
    rhs_ref, w_ref, sol_ref, res_ref,
    raw, w0, f0, cr0, g0, big0, a0, b0, x0, s0,
    w1, f1, rc1, cr1, g1, big1, a1, b1, t1,
    w2, f2, rc2, cr2, g2, x2, big2, a2, b2, t2,
    w3, f3, rc3, cr3, g3row, g3, c3, t3,
    f4, rc4, tmp, dummy, dummy1, w0x,
    load_sem, send_sem, recv_sem, all_send, all_recv,
):
    b = lax.axis_index("blk")
    g = lax.axis_index("grp")

    loads = [pltpu.make_async_copy(w_ref.at[k], raw.at[k], load_sem.at[k]) for k in range(6)]
    loads.append(pltpu.make_async_copy(rhs_ref, raw.at[6], load_sem.at[6]))
    for copy in loads:
        copy.start()

    def device(dx, dy):
        return (lax.rem(b + dx + BLK, BLK), lax.rem(g + dy + GRP, GRP))

    barrier = pltpu.get_barrier_semaphore()

    def greet(dx, dy):
        pl.semaphore_signal(barrier, inc=1, device_id=device(dx, dy), device_id_type=MESH)

    def greet_block(dx, carry):
        for dy in range(GRP):
            greet(dx, dy)
        return carry

    for dy in range(1, GRP):
        greet(0, dy)
    lax.fori_loop(1, BLK, greet_block, 0)

    def loop(begin, end, step):
        def one(index, carry):
            step(index)
            return carry

        lax.fori_loop(begin, end, one, 0)

    def patch(view, lead, fields, level, dx, dy, layers_x, layers_y, into=None):
        into = view if into is None else into
        size, start_x, start_y = level
        sx, tx = piece(dx, size, start_x, *layers_x)
        sy, ty = piece(dy, size, start_y, *layers_y)
        rows = fields * (layers_x[1] if dx else size) * (layers_y[1] if dy else size)
        return view.at[lead + (sx, sy)], into.at[lead + (tx, ty)], device(dx, dy), rows

    def faces(view, lead, fields, level, layers, into=None):
        return [patch(view, lead, fields, level, dx, dy, layers, layers, into) for dx, dy in FACES]

    def corners(view, lead, fields, level, layers_x, layers_y, into=None):
        return [
            patch(view, lead, fields, level, dx, dy, layers_x, layers_y, into) for dx, dy in CORNERS
        ]

    def inward(view, each, level, layer, into=None):
        return [
            patch(view, (pl.ds(k * each, each),), each, level, dx, dy, (layer, 1), (layer, 1), into)
            for k, (dx, dy) in enumerate(FACES)
        ]

    batches = []

    def batch(parts):
        index = len(batches)
        copies = [
            pltpu.make_async_remote_copy(
                src_ref=src,
                dst_ref=dst,
                send_sem=send_sem.at[index],
                recv_sem=recv_sem.at[index],
                device_id=to,
                device_id_type=MESH,
            )
            for src, dst, to, _ in parts
        ]
        rows = sum(part[3] for part in parts)
        batches.append((copies, dummy.at[pl.ds(0, rows)], index))
        return batches[-1]

    def start(one):
        for copy in one[0]:
            copy.start()

    def arrived(one):
        pltpu.make_async_copy(one[1], one[1], recv_sem.at[one[2]]).wait()

    def departed(one):
        pltpu.make_async_copy(one[1], one[1], send_sem.at[one[2]]).wait()

    def spread(src, dst, offsets, slot):
        for dx, dy in offsets:
            pltpu.make_async_remote_copy(
                src_ref=src,
                dst_ref=dst,
                send_sem=all_send.at[slot],
                recv_sem=all_recv.at[slot],
                device_id=device(dx, dy),
                device_id_type=MESH,
            ).start()

    def spread_all(c):
        row, mine = g3row.at[c], g3.at[c, b, pl.ds(g, 1), :]
        pltpu.make_async_copy(row, mine, all_recv.at[2 + c]).start()
        spread(row, mine, EVERYONE, 2 + c)

    def wait_for(ref, sem):
        pltpu.make_async_copy(ref, ref, sem).wait()

    def inside(rows, size, start_x, start_y):
        def mask(p, n):
            shape = (n, rows, 128)
            x = lax.broadcasted_iota(jnp.int32, shape, 0) + (b * size + p - start_x)
            y = lax.broadcasted_iota(jnp.int32, shape, 1) + (g * size - start_y)
            ok_x = jnp.logical_and(x >= 0, x < BLK * size)
            ok_y = jnp.logical_and(y >= 0, y < GRP * size)
            return jnp.logical_and(ok_x, ok_y)

        return mask

    def planes(begin, end, size, step):
        count = (end - begin) // size
        if count == 1:
            step(begin, size)
        elif count > 1:
            loop(0, count, lambda i: step(begin + i * size, size))
        if end - begin > count * size:
            step(begin + count * size, end - begin - count * size)

    def pairs(v):
        both = v.reshape((v.shape[0] // 2, 2) + v.shape[1:])
        return both[:, 0] + both[:, 1]

    def doubled(v):
        wide = jnp.broadcast_to(v[:, None], (v.shape[0], 2) + v.shape[1:])
        return wide.reshape((2 * v.shape[0],) + v.shape[1:])

    zi = lax.broadcasted_iota(jnp.int32, (256, 256), 0)
    ci = lax.broadcasted_iota(jnp.int32, (256, 256), 1)
    parted = jnp.where(ci < 128, 2 * ci, 2 * ci - 255)
    split = jnp.where(zi == parted, 1.0, 0.0).astype(jnp.bfloat16)

    def part_weights(i):
        first = 3 * i
        for k in range(3):
            pltpu.make_async_copy(w_ref.at[first + k], raw.at[first + k], load_sem.at[first + k]).wait()
        both = split_dot(raw[pl.ds(first, 3)].reshape(768, 256), split).reshape(3, 16, 16, 256)
        for k in range(3):
            for part in range(2):
                w0[2 * (first + k) + part, 4:20, 4:20, :] = both[k, :, :, 128 * part : 128 * part + 128]

    loop(0, 2, part_weights)
    loads[6].wait()
    both = split_dot(raw[6].reshape(256, 256), split)
    for part in range(2):
        total = w0[part, 4:20, 4:20, :]
        for k in range(1, 6):
            total = total + w0[2 * k + part, 4:20, 4:20, :]
        source = both[:, 128 * part : 128 * part + 128].reshape(16, 16, 128)
        g0[0, part, 4:20, 4:20, :] = (OMEGA / total) * source

    pl.semaphore_wait(barrier, BLK * GRP - 1)

    every = slice(None)
    level_0, level_1, level_2 = (16, 4, 4), (8, 6, 8), (4, 4, 4)

    def halo(view, lead, fields, level, layers, corner):
        return faces(view, lead, fields, level, (1, layers)) + corners(
            view, lead, fields, level, (1, corner), (1, corner)
        )

    cycles = range(CYCLES)
    g0_halo = [batch(halo(g0, (c, every), 2, level_0, 2, 1)) for c in cycles]
    g1_halo = [batch(halo(g1, (c,), 1, level_1, 6, 5)) for c in cycles]
    x0_halo = [batch(halo(x0, (c, every), 2, level_0, 3, 2)) for c in cycles]
    x2_halo = [batch(halo(x2, (c, every), 2, level_2, 4, 4)) for c in cycles]
    w0_halo = batch(halo(w0, (every,), 12, level_0, 1, 1) + inward(w0, 2, level_0, 2))
    w0_rest = batch(
        faces(w0, (every,), 12, level_0, (2, 1), w0x)
        + corners(w0, (every,), 12, level_0, (1, 2), (1, 2), w0x)
        + inward(w0, 2, level_0, 3, w0x)
    )
    w1_halo = batch(
        halo(w1, (every,), 6, level_1, 5, 3)
        + inward(w1, 1, level_1, 6)
        + corners(w1, (every,), 6, level_1, (4, 2), (1, 2))
        + corners(w1, (every,), 6, level_1, (1, 2), (4, 2))
    )
    w2_halo = batch(halo(w2, (every,), 6, level_2, 3, 4) + inward(w2, 1, level_2, 4))

    start(g0_halo[0])
    start(w0_halo)

    def weights_1(k):
        total = None
        for part in range(2):
            for dy in range(2):
                term = pairs(w0[2 * k + part, 4:20, pl.ds(4 + dy, 8, stride=2), :])
                total = term if total is None else total + term
        w1[k, 6:14, 8:16, :] = total * (1.0 / 32.0)

    loop(0, 6, weights_1)
    start(w1_halo)
    total = w1[0, 6:14, 8:16, :]
    for k in range(1, 6):
        total = total + w1[k, 6:14, 8:16, :]
    rc1[...] = OMEGA / total
    for k in range(6):
        total = None
        for dy in range(2):
            term = pairs(w1[k, 6:14, pl.ds(8 + dy, 4, stride=2), :])
            total = term if total is None else total + term
        w2[k, 4:8, 4:8, :] = (total + lane_swap(total, 1)) * (1.0 / 32.0)

    quad = lane_index((1, 128)) & 3

    def pack_quads(cells):
        out = cells[3]
        for n in range(3):
            out = jnp.where(quad == n, cells[n], out)
        return out

    for k in range(6):
        total = pairs(w2[k, 4:8, 4:8, :])
        total = (total + lane_swap(total, 2)) * (1.0 / 32.0)
        cells = []
        for xl in range(2):
            for yl in range(2):
                cells.append(total[xl, 2 * yl : 2 * yl + 1] + total[xl, 2 * yl + 1 : 2 * yl + 2])
        w3[k, b, pl.ds(g, 1), :] = pack_quads(cells)
    mine = w3.at[:, b, pl.ds(g, 1), :]
    spread(mine, mine, [(0, dy) for dy in range(1, GRP)], 0)

    mask0 = inside(24, 16, 4, 4)
    mask1 = inside(24, 8, 6, 8)
    mask2 = inside(16, 4, 4, 4)

    def relaxed(total, mask):
        return jnp.where(mask, OMEGA / total, 0.0)

    arrived(w0_halo)

    def fold_0(p, n):
        here, low, high = pl.ds(p, n), pl.ds(p - 1, n), pl.ds(p + 1, n)
        mask = mask0(p, n)
        lanes = lane_index((n, 24, 128))
        rc = []
        for part in range(2):
            total = w0[part, here]
            for k in range(1, 6):
                total = total + w0[2 * k + part, here]
            rc.append(relaxed(total, mask))
            cr0[part, here] = total * (1.0 / OMEGA)
            f0[0 + part, here] = rc[part] * w0[0 + part, low]
            f0[2 + part, here] = rc[part] * w0[2 + part, high]
            f0[4 + part, here] = rc[part] * row_roll(w0[4 + part, here], 1)
            f0[6 + part, here] = rc[part] * row_roll(w0[6 + part, here], -1)
        f0[8, here] = rc[0] * jnp.where(lanes == 0, 0.0, lane_roll(w0[9, here], 1))
        f0[9, here] = rc[1] * w0[8, here]
        f0[10, here] = rc[0] * w0[11, here]
        f0[11, here] = rc[1] * jnp.where(lanes == 127, 0.0, lane_roll(w0[10, here], -1))

    planes(3, 21, 6, fold_0)

    def merge_0():
        for x in (2, 21):
            w0[:, x, 4:20, :] = w0x[:, x, 4:20, :]
        for y in (2, 21):
            w0[:, 4:20, y : y + 1, :] = w0x[:, 4:20, y : y + 1, :]
        for x in (2, 20):
            for y in (2, 20):
                w0[:, x : x + 2, y : y + 2, :] = w0x[:, x : x + 2, y : y + 2, :]
        w0[0:2, 1, 4:20, :] = w0x[0:2, 1, 4:20, :]
        w0[2:4, 22, 4:20, :] = w0x[2:4, 22, 4:20, :]
        w0[4:6, 4:20, 1:2, :] = w0x[4:6, 4:20, 1:2, :]
        w0[6:8, 4:20, 22:23, :] = w0x[6:8, 4:20, 22:23, :]

    def sweep_0(u, p, n):
        here, low, high = pl.ds(p, n), pl.ds(p - 1, n), pl.ds(p + 1, n)
        e, o = u[0, here], u[1, here]
        out_e = KEEP * e + big0[0, here]
        out_o = KEEP * o + big0[1, here]
        out_e += f0[0, here] * u[0, low]
        out_o += f0[1, here] * u[1, low]
        out_e += f0[2, here] * u[0, high]
        out_o += f0[3, here] * u[1, high]
        out_e += f0[4, here] * row_roll(e, 1)
        out_o += f0[5, here] * row_roll(o, 1)
        out_e += f0[6, here] * row_roll(e, -1)
        out_o += f0[7, here] * row_roll(o, -1)
        out_e += f0[8, here] * lane_roll(o, 1)
        out_o += f0[9, here] * e
        out_e += f0[10, here] * o
        out_o += f0[11, here] * lane_roll(e, -1)
        return out_e, out_o

    def sweep_c(u, big, f, p, n, step):
        here = pl.ds(p, n)
        v = u[here]
        out = KEEP * v + big[here]
        out += f[0, here] * u[pl.ds(p - 1, n)]
        out += f[1, here] * u[pl.ds(p + 1, n)]
        out += f[2, here] * row_roll(v, 1)
        out += f[3, here] * row_roll(v, -1)
        out += f[4, here] * lane_roll(v, step)
        out += f[5, here] * lane_roll(v, -step)
        return out

    def fold_c(w, f, cr, p, n, step, mask):
        here = pl.ds(p, n)
        total = w[0, here]
        for k in range(1, 6):
            total = total + w[k, here]
        r = relaxed(total, mask)
        cr[here] = total * (1.0 / OMEGA)
        lanes = lane_index(r.shape)
        f[0, here] = r * w[0, pl.ds(p - 1, n)]
        f[1, here] = r * w[1, pl.ds(p + 1, n)]
        f[2, here] = r * row_roll(w[2, here], 1)
        f[3, here] = r * row_roll(w[3, here], -1)
        f[4, here] = r * jnp.where(lanes < step, 0.0, lane_roll(w[4, here], step))
        f[5, here] = r * jnp.where(lanes >= 128 - step, 0.0, lane_roll(w[5, here], -step))
        return r

    shape3 = (BLK, GRP, 128)

    def before(v):
        return jnp.concatenate([v[BLK - 1 :], v[: BLK - 1]], axis=0)

    def after(v):
        return jnp.concatenate([v[1:], v[:1]], axis=0)

    lane3 = lane_index(shape3)
    blk3 = lax.broadcasted_iota(jnp.int32, shape3, 0)
    grp3 = lax.broadcasted_iota(jnp.int32, shape3, 1)
    low_x = (lane3 & 2) == 0
    low_y = (lane3 & 1) == 0

    def shifts_3(v):
        moved = lane_roll(v, 2)
        yield moved
        yield after(moved)
        moved = lane_roll(v, -2)
        yield moved
        yield before(moved)
        moved = lane_roll(v, 1)
        yield moved
        yield row_roll(moved, -1)
        moved = lane_roll(v, -1)
        yield moved
        yield row_roll(moved, 1)
        yield lane_roll(v, 4)
        yield lane_roll(v, -4)

    def shifts_4(v):
        yield before(v)
        yield after(v)
        yield row_roll(v, 1)
        yield row_roll(v, -1)
        yield lane_roll(v, 8)
        yield lane_roll(v, -8)

    def octet(v):
        v = v + lane_swap(v, 1)
        v = v + lane_swap(v, 2)
        return v + lane_swap(v, 4)

    def fold_coarse():
        ws = [w3[k] for k in range(6)]
        total = ws[0] + ws[1] + ws[2] + ws[3] + ws[4] + ws[5]
        rc = OMEGA / total
        rc3[...] = rc
        cr3[...] = total * (1.0 / OMEGA)
        high_x, high_y = jnp.logical_not(low_x), jnp.logical_not(low_y)
        uses = (
            (0, high_x),
            (1, jnp.logical_and(high_x, blk3 < BLK - 1)),
            (1, low_x),
            (0, jnp.logical_and(low_x, blk3 > 0)),
            (2, high_y),
            (3, jnp.logical_and(high_y, grp3 < GRP - 1)),
            (3, low_y),
            (2, jnp.logical_and(low_y, grp3 > 0)),
            (4, lane3 >= 4),
            (5, lane3 < 124),
        )
        for n, (k, used) in enumerate(uses):
            moved = list(shifts_3(ws[k]))[n]
            f3[n] = jnp.where(used, rc * moved, 0.0)
        total = None
        for k in range(6):
            coarse = octet(ws[k]) * (1.0 / 32.0)
            f4[k] = coarse
            total = coarse if total is None else total + coarse
        rc = OMEGA / total
        rc4[...] = rc
        edge = (blk3 == 0, blk3 == BLK - 1, grp3 == 0, grp3 == GRP - 1, lane3 < 8, lane3 >= 120)
        for k in range(6):
            moved = list(shifts_4(f4[k]))[k]
            f4[k] = jnp.where(edge[k], 0.0, rc * moved)

    def sweep_3(v, big):
        out = KEEP * v + big
        for k, moved in enumerate(shifts_3(v)):
            out += f3[k] * moved
        return out

    def sweep_4(v, big):
        out = KEEP * v + big
        for k, moved in enumerate(shifts_4(v)):
            out += f4[k] * moved
        return out

    def coarse_levels(source):
        big = rc3[...] * source
        u = sweep_3(big, big)
        left = (sweep_3(u, big) - u) * cr3[...]
        big_4 = rc4[...] * (octet(left) * 0.125)
        v = lax.fori_loop(0, 7, lambda n, v: sweep_4(v, big_4), big_4, unroll=True)
        u = u + v
        u = sweep_3(u, big)
        return sweep_3(u, big)

    for c in range(CYCLES):
        arrived(g0_halo[c])

        def source_0(p, n):
            here = pl.ds(p, n)
            mask = mask0(p, n)
            for part in range(2):
                big0[part, here] = jnp.where(mask, g0[c, part, here], 0.0)

        planes(2, 22, 10, source_0)

        def down_0(p, n):
            here = pl.ds(p, n)
            a0[0, here], a0[1, here] = sweep_0(big0, p, n)

        planes(3, 21, 9, down_0)

        def restrict_0(p, n):
            here = pl.ds(p, n)
            e, o = sweep_0(a0, p, n)
            left = (e - a0[0, here]) * cr0[0, here] + (o - a0[1, here]) * cr0[1, here]
            m = n // 2
            tmp[0:m] = pairs(left)
            rows = tmp[0:m, pl.ds(4, 8, stride=2), :] + tmp[0:m, pl.ds(5, 8, stride=2), :]
            here = pl.ds(lax.div(p, 2) - 2, m)
            there = pl.ds(lax.div(p, 2) + 4, m)
            g1[c, there, 8:16, :] = rc1[here] * (rows * 0.125)

        planes(4, 20, 8, restrict_0)
        start(g1_halo[c])
        for part in range(2):
            x0[c, part, 4:20, 4:20, :] = a0[part, 4:20, 4:20, :]
        start(x0_halo[c])

        if c == 0:
            start(w2_halo)
            wait_for(w3.at[:, pl.ds(0, GRP - 1), pl.ds(0, 1), :], all_recv.at[0])
            block = w3.at[:, b]
            spread(block, block, [(dx, 0) for dx in range(1, BLK)], 1)
            start(w0_rest)
            arrived(w1_halo)
            planes(1, 19, 6, lambda p, n: fold_c(w1, f1, cr1, p, n, 1, mask1(p, n)))
        arrived(g1_halo[c])
        big1[...] = jnp.where(mask1(0, 20), g1[c], 0.0)
        a1[1:19] = sweep_c(big1, big1, f1, 1, 18, 1)
        left = (sweep_c(a1, big1, f1, 2, 16, 1) - a1[2:18]) * cr1[2:18]
        tmp[0:8] = pairs(left)
        rows = tmp[0:8, pl.ds(4, 8, stride=2), :] + tmp[0:8, pl.ds(5, 8, stride=2), :]
        g2[2:10, 2:10, :] = (rows + lane_swap(rows, 1)) * 0.125
        if c == 0:
            arrived(w2_halo)
            rc2[1:11] = fold_c(w2, f2, cr2, 1, 10, 2, mask2(1, 10))
        big2[2:10] = rc2[2:10] * g2[2:10]
        a2[3:9] = sweep_c(big2, big2, f2, 3, 6, 2)
        left = (sweep_c(a2, big2, f2, 4, 4, 2) - a2[4:8]) * cr2[4:8]
        left = pairs(left)
        tmp[0:2, 0:16, :] = (left + lane_swap(left, 2)) * 0.125
        cells = []
        for xl in range(2):
            for yl in range(2):
                cells.append(tmp[xl, pl.ds(4 + 2 * yl, 1), :] + tmp[xl, pl.ds(5 + 2 * yl, 1), :])
        g3row[c] = pack_quads(cells)
        spread_all(c)
        x2[c, 0, 4:8, 4:8, :] = big2[4:8, 4:8, :]
        x2[c, 1, 4:8, 4:8, :] = a2[4:8, 4:8, :]
        start(x2_halo[c])
        if c == 0:
            wait_for(w3.at[:, pl.ds(0, BLK - 1)], all_recv.at[1])
            fold_coarse()
            arrived(w0_rest)
            merge_0()
            planes(2, 22, 5, fold_0)
        wait_for(g3.at[c], all_recv.at[2 + c])
        c3[1:17] = coarse_levels(g3[c])

        near = c3[pl.ds(b, 3)]
        quads = lane_index((3, 8, 128)) & 3
        for xl in range(2):
            for yl in range(2):
                own = jnp.where(quads == 2 * xl + yl, near, 0.0)
                own = own + lane_swap(own, 1)
                own = own + lane_swap(own, 2)
                for dy in range(2):
                    t3[:, xl, pl.ds(8 + 2 * yl + dy, 8, stride=4), :] = own
        arrived(x2_halo[c])
        inside_2 = mask2(0, 12)
        big2[...] = jnp.where(inside_2, x2[c, 0], 0.0)
        add = doubled(t3[:, :, pl.ds(4 + 4 * g, 16), :].reshape(6, 16, 128))
        b2[...] = jnp.where(inside_2, x2[c, 1] + add, 0.0)
        a2[1:11] = sweep_c(b2, big2, f2, 1, 10, 2)
        t2[...] = sweep_c(a2, big2, f2, 2, 8, 2)
        rows = t2[:, 2:10, :]
        t1[:, pl.ds(4, 8, stride=2), :] = rows
        t1[:, pl.ds(5, 8, stride=2), :] = rows

        b1[2:18] = jnp.where(mask1(2, 16), a1[2:18] + doubled(t1[...]), 0.0)
        a1[3:17] = sweep_c(b1, big1, f1, 3, 14, 1)
        tmp[...] = sweep_c(a1, big1, f1, 4, 12, 1)
        rows = tmp[:, 6:18, :]
        s0[:, pl.ds(0, 12, stride=2), :] = rows
        s0[:, pl.ds(1, 12, stride=2), :] = rows

        arrived(x0_halo[c])

        def correct_0(p, n):
            here = pl.ds(p, n)
            add = doubled(s0[pl.ds(lax.div(p, 2), n // 2)])
            mask = mask0(p, n)
            for part in range(2):
                b0[part, here] = jnp.where(mask, x0[c, part, here] + add, 0.0)

        planes(0, 24, 8, correct_0)

        def up_0a(p, n):
            here = pl.ds(p, n)
            a0[0, here], a0[1, here] = sweep_0(b0, p, n)

        planes(2, 22, 10, up_0a)

        def up_0b(p, n):
            here = pl.ds(p, n)
            b0[0, here], b0[1, here] = sweep_0(a0, p, n)

        planes(3, 21, 9, up_0b)

        def update(p, n):
            here, out = pl.ds(p, n), pl.ds(p - 4, n)
            swept = sweep_0(b0, p, n)
            for part in range(2):
                lanes = pl.ds(128 * part, 128)
                u = b0[part, here]
                change = swept[part] - u
                if c + 1 < CYCLES:
                    g0[c + 1, part, here, 4:20, :] = change[:, 4:20, :]
                else:
                    res_ref[out, :, lanes] = (change * cr0[part, here])[:, 4:20, :]
                u = u[:, 4:20, :]
                sol_ref[out, :, lanes] = u if c == 0 else sol_ref[out, :, lanes] + u

        planes(4, 20, 8, update)
        if c + 1 < CYCLES:
            start(g0_halo[c + 1])

    for one in batches:
        departed(one)
    wait_for(w3.at[:, pl.ds(0, GRP - 1), pl.ds(0, 1), :], all_send.at[0])
    wait_for(w3.at[:, pl.ds(0, BLK - 1)], all_send.at[1])
    for c in cycles:
        wait_for(dummy1, all_send.at[2 + c])


def join_kernel(sol_in, res_in, sol_out, res_out, halves, whole, load_sem, store_sem):
    loads = [pltpu.make_async_copy(ref, halves.at[n], load_sem.at[n]) for n, ref in enumerate((sol_in, res_in))]
    stores = [pltpu.make_async_copy(whole.at[n], ref, store_sem.at[n]) for n, ref in enumerate((sol_out, res_out))]
    for copy in loads:
        copy.start()
    zi = lax.broadcasted_iota(jnp.int32, (256, 256), 1)
    ci = lax.broadcasted_iota(jnp.int32, (256, 256), 0)
    parted = jnp.where(ci < 128, 2 * ci, 2 * ci - 255)
    joined = jnp.where(zi == parted, 1.0, 0.0).astype(jnp.bfloat16)
    for n in range(2):
        loads[n].wait()
        whole[n] = split_dot(halves[n].reshape(256, 256), joined).reshape(16, 16, 256)
        stores[n].start()
    for copy in stores:
        copy.wait()


def body(right_side, weights):
    vmem = pl.BlockSpec(memory_space=pltpu.VMEM)
    field = jax.ShapeDtypeStruct((16, 16, 256), F32)
    f0 = (24, 24, 128)
    f1 = (20, 24, 128)
    f2 = (12, 16, 128)
    f3 = (BLK, GRP, 128)

    def buf(*shape):
        return pltpu.VMEM(shape, F32)

    parted = pl.pallas_call(
        kernel,
        out_shape=(field, field),
        in_specs=[pl.BlockSpec(memory_space=pl.ANY)] * 2,
        out_specs=(vmem, vmem),
        scratch_shapes=[
            buf(7, 16, 16, 256),
            buf(12, *f0), buf(12, *f0), buf(2, *f0), buf(2, 2, *f0), buf(2, *f0),
            buf(2, *f0), buf(2, *f0), buf(2, 2, *f0), buf(12, 24, 128),
            buf(6, *f1), buf(6, *f1), buf(8, 8, 128), buf(*f1), buf(2, *f1), buf(*f1), buf(*f1), buf(*f1), buf(8, 24, 128),
            buf(6, *f2), buf(6, *f2), buf(*f2), buf(*f2), buf(*f2), buf(2, 2, *f2), buf(*f2), buf(*f2), buf(*f2),
            buf(8, 16, 128),
            buf(6, *f3), buf(10, *f3), buf(*f3), buf(*f3), buf(2, 1, 128), buf(2, *f3),
            buf(18, 8, 128), buf(3, 2, 48, 128),
            buf(6, *f3), buf(*f3), buf(12, 24, 128), buf(2048, 128), buf(127, 1, 128), buf(12, *f0),
            pltpu.SemaphoreType.DMA((7,)),
            pltpu.SemaphoreType.DMA((12,)),
            pltpu.SemaphoreType.DMA((12,)),
            pltpu.SemaphoreType.DMA((4,)),
            pltpu.SemaphoreType.DMA((4,)),
        ],
        compiler_params=pltpu.CompilerParams(
            collective_id=0, has_side_effects=True, vmem_limit_bytes=56 * 1024 * 1024
        ),
    )(right_side, weights)
    return pl.pallas_call(
        join_kernel,
        out_shape=(field, field),
        in_specs=[pl.BlockSpec(memory_space=pltpu.HBM)] * 2,
        out_specs=[pl.BlockSpec(memory_space=pltpu.HBM)] * 2,
        scratch_shapes=[
            buf(2, 16, 16, 256), buf(2, 16, 16, 256), pltpu.SemaphoreType.DMA((2,)), pltpu.SemaphoreType.DMA((2,)),
        ],
        compiler_params=pltpu.CompilerParams(vmem_limit_bytes=60 * 1024 * 1024),
    )(*parted)


def solution(mesh):
    return jax.shard_map(
        body,
        mesh=mesh,
        in_specs=(P("blk", "grp", None), P(None, "blk", "grp", None)),
        out_specs=(P("blk", "grp", None), P("blk", "grp", None)),
        check_vma=False,
    )
```

```python
import functools

import jax
import jax.numpy as jnp
from jax import lax
from jax.experimental import pallas as pl
from jax.experimental.pallas import tpu as pltpu
from jax.sharding import PartitionSpec as P

MESH = pl.DeviceIdType.MESH
F32 = jnp.float32
BLK, GRP = 16, 8
OMEGA = 0.7
KEEP = 1.0 - OMEGA
FACES = ((1, 0), (-1, 0), (0, 1), (0, -1))
CORNERS = ((1, 1), (1, -1), (-1, 1), (-1, -1))


def distance(offset):
    dx, dy = offset
    x, y, z = dx % 4, dy // 2, dx // 4
    return min(x, 4 - x) + min(y, 4 - y) + min(z, 4 - z)


EVERYONE = sorted(((dx, dy) for dx in range(BLK) for dy in range(GRP) if dx or dy), key=distance, reverse=True)
CYCLES = 2


def lane_roll(v, n):
    return pltpu.roll(v, n % 128, v.ndim - 1)


def row_roll(v, n):
    axis = v.ndim - 2
    return pltpu.roll(v, n % v.shape[axis], axis)


def lane_index(shape):
    return lax.broadcasted_iota(jnp.int32, shape, len(shape) - 1)


def lane_swap(v, n):
    even = (lane_index(v.shape[-2:]) & n) == 0
    even = jnp.broadcast_to(even, v.shape)
    return jnp.where(even, lane_roll(v, -n), lane_roll(v, n))


def split_dot(x, matrix):
    high = x.astype(jnp.bfloat16)
    rest = x - high.astype(F32)
    middle = rest.astype(jnp.bfloat16)
    low = (rest - middle.astype(F32)).astype(jnp.bfloat16)
    dot = functools.partial(jnp.dot, preferred_element_type=F32)
    return (dot(low, matrix) + dot(middle, matrix)) + dot(high, matrix)


def piece(delta, size, start, first, count):
    if delta == 1:
        return pl.ds(start + size + 1 - first - count, count), pl.ds(start + 1 - first - count, count)
    if delta == -1:
        return pl.ds(start + first - 1, count), pl.ds(start + size + first - 1, count)
    return pl.ds(start, size), pl.ds(start, size)


def kernel(
    rhs_ref, w_ref, sol_ref, res_ref,
    raw, w0, f0, cr0, g0, big0, a0, b0, x0, s0,
    w1, f1, rc1, cr1, g1, big1, a1, b1, t1,
    w2, f2, rc2, cr2, g2, x2, big2, a2, b2, t2,
    w3, f3, rc3, cr3, g3row, g3, c3, t3,
    f4, rc4, tmp, dummy, dummy1, w0x,
    load_sem, send_sem, recv_sem, all_send, all_recv,
):
    b = lax.axis_index("blk")
    g = lax.axis_index("grp")

    loads = [pltpu.make_async_copy(w_ref.at[k], raw.at[k], load_sem.at[k]) for k in range(6)]
    loads.append(pltpu.make_async_copy(rhs_ref, raw.at[6], load_sem.at[6]))
    for copy in loads:
        copy.start()

    def device(dx, dy):
        return (lax.rem(b + dx + BLK, BLK), lax.rem(g + dy + GRP, GRP))

    barrier = pltpu.get_barrier_semaphore()

    def greet(dx, dy):
        pl.semaphore_signal(barrier, inc=1, device_id=device(dx, dy), device_id_type=MESH)

    def greet_block(dx, carry):
        for dy in range(GRP):
            greet(dx, dy)
        return carry

    for dy in range(1, GRP):
        greet(0, dy)
    lax.fori_loop(1, BLK, greet_block, 0)

    def loop(begin, end, step):
        def one(index, carry):
            step(index)
            return carry

        lax.fori_loop(begin, end, one, 0)

    def patch(view, lead, fields, level, dx, dy, layers_x, layers_y, into=None):
        into = view if into is None else into
        size, start_x, start_y = level
        sx, tx = piece(dx, size, start_x, *layers_x)
        sy, ty = piece(dy, size, start_y, *layers_y)
        rows = fields * (layers_x[1] if dx else size) * (layers_y[1] if dy else size)
        return view.at[lead + (sx, sy)], into.at[lead + (tx, ty)], device(dx, dy), rows

    def faces(view, lead, fields, level, layers, into=None):
        return [patch(view, lead, fields, level, dx, dy, layers, layers, into) for dx, dy in FACES]

    def corners(view, lead, fields, level, layers_x, layers_y, into=None):
        return [
            patch(view, lead, fields, level, dx, dy, layers_x, layers_y, into) for dx, dy in CORNERS
        ]

    def inward(view, each, level, layer, into=None):
        return [
            patch(view, (pl.ds(k * each, each),), each, level, dx, dy, (layer, 1), (layer, 1), into)
            for k, (dx, dy) in enumerate(FACES)
        ]

    batches = []

    def batch(parts):
        index = len(batches)
        copies = [
            pltpu.make_async_remote_copy(
                src_ref=src,
                dst_ref=dst,
                send_sem=send_sem.at[index],
                recv_sem=recv_sem.at[index],
                device_id=to,
                device_id_type=MESH,
            )
            for src, dst, to, _ in parts
        ]
        rows = sum(part[3] for part in parts)
        batches.append((copies, dummy.at[pl.ds(0, rows)], index))
        return batches[-1]

    def start(one):
        for copy in one[0]:
            copy.start()

    def arrived(one):
        pltpu.make_async_copy(one[1], one[1], recv_sem.at[one[2]]).wait()

    def departed(one):
        pltpu.make_async_copy(one[1], one[1], send_sem.at[one[2]]).wait()

    def spread(src, dst, offsets, slot):
        for dx, dy in offsets:
            pltpu.make_async_remote_copy(
                src_ref=src,
                dst_ref=dst,
                send_sem=all_send.at[slot],
                recv_sem=all_recv.at[slot],
                device_id=device(dx, dy),
                device_id_type=MESH,
            ).start()

    def spread_all(c):
        row, mine = g3row.at[c], g3.at[c, b, pl.ds(g, 1), :]
        pltpu.make_async_copy(row, mine, all_recv.at[2 + c]).start()
        spread(row, mine, EVERYONE, 2 + c)

    def wait_for(ref, sem):
        pltpu.make_async_copy(ref, ref, sem).wait()

    def inside(rows, size, start_x, start_y):
        def mask(p, n):
            shape = (n, rows, 128)
            x = lax.broadcasted_iota(jnp.int32, shape, 0) + (b * size + p - start_x)
            y = lax.broadcasted_iota(jnp.int32, shape, 1) + (g * size - start_y)
            ok_x = jnp.logical_and(x >= 0, x < BLK * size)
            ok_y = jnp.logical_and(y >= 0, y < GRP * size)
            return jnp.logical_and(ok_x, ok_y)

        return mask

    def planes(begin, end, size, step):
        count = (end - begin) // size
        if count == 1:
            step(begin, size)
        elif count > 1:
            loop(0, count, lambda i: step(begin + i * size, size))
        if end - begin > count * size:
            step(begin + count * size, end - begin - count * size)

    def pairs(v):
        both = v.reshape((v.shape[0] // 2, 2) + v.shape[1:])
        return both[:, 0] + both[:, 1]

    def doubled(v):
        wide = jnp.broadcast_to(v[:, None], (v.shape[0], 2) + v.shape[1:])
        return wide.reshape((2 * v.shape[0],) + v.shape[1:])

    zi = lax.broadcasted_iota(jnp.int32, (256, 256), 0)
    ci = lax.broadcasted_iota(jnp.int32, (256, 256), 1)
    parted = jnp.where(ci < 128, 2 * ci, 2 * ci - 255)
    split = jnp.where(zi == parted, 1.0, 0.0).astype(jnp.bfloat16)

    def part_weights(i):
        first = 3 * i
        for k in range(3):
            pltpu.make_async_copy(w_ref.at[first + k], raw.at[first + k], load_sem.at[first + k]).wait()
        both = split_dot(raw[pl.ds(first, 3)].reshape(768, 256), split).reshape(3, 16, 16, 256)
        for k in range(3):
            for part in range(2):
                w0[2 * (first + k) + part, 4:20, 4:20, :] = both[k, :, :, 128 * part : 128 * part + 128]

    loop(0, 2, part_weights)

    pl.semaphore_wait(barrier, BLK * GRP - 1)

    every = slice(None)
    level_0, level_1, level_2 = (16, 4, 4), (8, 6, 8), (4, 4, 4)

    def halo(view, lead, fields, level, layers, corner):
        return corners(view, lead, fields, level, (1, corner), (1, corner)) + faces(
            view, lead, fields, level, (1, layers)
        )

    cycles = range(CYCLES)
    g0_halo = [batch(halo(g0, (c, every), 2, level_0, 2, 1)) for c in cycles]
    g1_halo = [batch(halo(g1, (c,), 1, level_1, 6, 5)) for c in cycles]
    x0_halo = [batch(halo(x0, (c, every), 2, level_0, 3, 2)) for c in cycles]
    x2_halo = [batch(halo(x2, (c, every), 2, level_2, 4, 4)) for c in cycles]
    w0_halo = batch(halo(w0, (every,), 12, level_0, 1, 1) + inward(w0, 2, level_0, 2))
    w0_rest = batch(
        faces(w0, (every,), 12, level_0, (2, 1), w0x)
        + corners(w0, (every,), 12, level_0, (1, 2), (1, 2), w0x)
        + inward(w0, 2, level_0, 3, w0x)
    )
    w1_halo = batch(
        halo(w1, (every,), 6, level_1, 5, 3)
        + inward(w1, 1, level_1, 6)
        + corners(w1, (every,), 6, level_1, (4, 2), (1, 2))
        + corners(w1, (every,), 6, level_1, (1, 2), (4, 2))
    )
    w2_halo = batch(halo(w2, (every,), 6, level_2, 3, 4) + inward(w2, 1, level_2, 4))

    start(w0_halo)
    loads[6].wait()
    both = split_dot(raw[6].reshape(256, 256), split)
    for part in range(2):
        total = w0[part, 4:20, 4:20, :]
        for k in range(1, 6):
            total = total + w0[2 * k + part, 4:20, 4:20, :]
        source = both[:, 128 * part : 128 * part + 128].reshape(16, 16, 128)
        g0[0, part, 4:20, 4:20, :] = (OMEGA / total) * source
    start(g0_halo[0])

    def weights_1(k):
        total = None
        for part in range(2):
            for dy in range(2):
                term = pairs(w0[2 * k + part, 4:20, pl.ds(4 + dy, 8, stride=2), :])
                total = term if total is None else total + term
        w1[k, 6:14, 8:16, :] = total * (1.0 / 32.0)

    loop(0, 6, weights_1)
    start(w1_halo)
    total = w1[0, 6:14, 8:16, :]
    for k in range(1, 6):
        total = total + w1[k, 6:14, 8:16, :]
    rc1[...] = OMEGA / total
    for k in range(6):
        total = None
        for dy in range(2):
            term = pairs(w1[k, 6:14, pl.ds(8 + dy, 4, stride=2), :])
            total = term if total is None else total + term
        w2[k, 4:8, 4:8, :] = (total + lane_swap(total, 1)) * (1.0 / 32.0)

    quad = lane_index((1, 128)) & 3

    def pack_quads(cells):
        out = cells[3]
        for n in range(3):
            out = jnp.where(quad == n, cells[n], out)
        return out

    for k in range(6):
        total = pairs(w2[k, 4:8, 4:8, :])
        total = (total + lane_swap(total, 2)) * (1.0 / 32.0)
        cells = []
        for xl in range(2):
            for yl in range(2):
                cells.append(total[xl, 2 * yl : 2 * yl + 1] + total[xl, 2 * yl + 1 : 2 * yl + 2])
        w3[k, b, pl.ds(g, 1), :] = pack_quads(cells)
    mine = w3.at[:, b, pl.ds(g, 1), :]
    spread(mine, mine, [(0, dy) for dy in range(1, GRP)], 0)

    mask0 = inside(24, 16, 4, 4)
    mask1 = inside(24, 8, 6, 8)
    mask2 = inside(16, 4, 4, 4)

    def relaxed(total, mask):
        return jnp.where(mask, OMEGA / total, 0.0)

    arrived(w0_halo)

    def fold_0(p, n):
        here, low, high = pl.ds(p, n), pl.ds(p - 1, n), pl.ds(p + 1, n)
        mask = mask0(p, n)
        lanes = lane_index((n, 24, 128))
        rc = []
        for part in range(2):
            total = w0[part, here]
            for k in range(1, 6):
                total = total + w0[2 * k + part, here]
            rc.append(relaxed(total, mask))
            cr0[part, here] = total * (1.0 / OMEGA)
            f0[0 + part, here] = rc[part] * w0[0 + part, low]
            f0[2 + part, here] = rc[part] * w0[2 + part, high]
            f0[4 + part, here] = rc[part] * row_roll(w0[4 + part, here], 1)
            f0[6 + part, here] = rc[part] * row_roll(w0[6 + part, here], -1)
        f0[8, here] = rc[0] * jnp.where(lanes == 0, 0.0, lane_roll(w0[9, here], 1))
        f0[9, here] = rc[1] * w0[8, here]
        f0[10, here] = rc[0] * w0[11, here]
        f0[11, here] = rc[1] * jnp.where(lanes == 127, 0.0, lane_roll(w0[10, here], -1))

    planes(3, 21, 9, fold_0)

    def merge_0():
        for x in (2, 21):
            w0[:, x, 4:20, :] = w0x[:, x, 4:20, :]
        for y in (2, 21):
            w0[:, 4:20, y : y + 1, :] = w0x[:, 4:20, y : y + 1, :]
        for x in (2, 20):
            for y in (2, 20):
                w0[:, x : x + 2, y : y + 2, :] = w0x[:, x : x + 2, y : y + 2, :]
        w0[0:2, 1, 4:20, :] = w0x[0:2, 1, 4:20, :]
        w0[2:4, 22, 4:20, :] = w0x[2:4, 22, 4:20, :]
        w0[4:6, 4:20, 1:2, :] = w0x[4:6, 4:20, 1:2, :]
        w0[6:8, 4:20, 22:23, :] = w0x[6:8, 4:20, 22:23, :]

    def sweep_0(u, p, n):
        here, low, high = pl.ds(p, n), pl.ds(p - 1, n), pl.ds(p + 1, n)
        e, o = u[0, here], u[1, here]
        out_e = KEEP * e + big0[0, here]
        out_o = KEEP * o + big0[1, here]
        out_e += f0[0, here] * u[0, low]
        out_o += f0[1, here] * u[1, low]
        out_e += f0[2, here] * u[0, high]
        out_o += f0[3, here] * u[1, high]
        out_e += f0[4, here] * row_roll(e, 1)
        out_o += f0[5, here] * row_roll(o, 1)
        out_e += f0[6, here] * row_roll(e, -1)
        out_o += f0[7, here] * row_roll(o, -1)
        out_e += f0[8, here] * lane_roll(o, 1)
        out_o += f0[9, here] * e
        out_e += f0[10, here] * o
        out_o += f0[11, here] * lane_roll(e, -1)
        return out_e, out_o

    def sweep_c(u, big, f, p, n, step):
        here = pl.ds(p, n)
        v = u[here]
        out = KEEP * v + big[here]
        out += f[0, here] * u[pl.ds(p - 1, n)]
        out += f[1, here] * u[pl.ds(p + 1, n)]
        out += f[2, here] * row_roll(v, 1)
        out += f[3, here] * row_roll(v, -1)
        out += f[4, here] * lane_roll(v, step)
        out += f[5, here] * lane_roll(v, -step)
        return out

    def fold_c(w, f, cr, p, n, step, mask):
        here = pl.ds(p, n)
        total = w[0, here]
        for k in range(1, 6):
            total = total + w[k, here]
        r = relaxed(total, mask)
        cr[here] = total * (1.0 / OMEGA)
        lanes = lane_index(r.shape)
        f[0, here] = r * w[0, pl.ds(p - 1, n)]
        f[1, here] = r * w[1, pl.ds(p + 1, n)]
        f[2, here] = r * row_roll(w[2, here], 1)
        f[3, here] = r * row_roll(w[3, here], -1)
        f[4, here] = r * jnp.where(lanes < step, 0.0, lane_roll(w[4, here], step))
        f[5, here] = r * jnp.where(lanes >= 128 - step, 0.0, lane_roll(w[5, here], -step))
        return r

    shape3 = (BLK, GRP, 128)

    def before(v):
        return jnp.concatenate([v[BLK - 1 :], v[: BLK - 1]], axis=0)

    def after(v):
        return jnp.concatenate([v[1:], v[:1]], axis=0)

    lane3 = lane_index(shape3)
    blk3 = lax.broadcasted_iota(jnp.int32, shape3, 0)
    grp3 = lax.broadcasted_iota(jnp.int32, shape3, 1)
    low_x = (lane3 & 2) == 0
    low_y = (lane3 & 1) == 0

    def shifts_3(v):
        moved = lane_roll(v, 2)
        yield moved
        yield after(moved)
        moved = lane_roll(v, -2)
        yield moved
        yield before(moved)
        moved = lane_roll(v, 1)
        yield moved
        yield row_roll(moved, -1)
        moved = lane_roll(v, -1)
        yield moved
        yield row_roll(moved, 1)
        yield lane_roll(v, 4)
        yield lane_roll(v, -4)

    def shifts_4(v):
        yield before(v)
        yield after(v)
        yield row_roll(v, 1)
        yield row_roll(v, -1)
        yield lane_roll(v, 8)
        yield lane_roll(v, -8)

    def octet(v):
        v = v + lane_swap(v, 1)
        v = v + lane_swap(v, 2)
        return v + lane_swap(v, 4)

    def fold_coarse():
        ws = [w3[k] for k in range(6)]
        total = ws[0] + ws[1] + ws[2] + ws[3] + ws[4] + ws[5]
        rc = OMEGA / total
        rc3[...] = rc
        cr3[...] = total * (1.0 / OMEGA)
        high_x, high_y = jnp.logical_not(low_x), jnp.logical_not(low_y)
        uses = (
            (0, high_x),
            (1, jnp.logical_and(high_x, blk3 < BLK - 1)),
            (1, low_x),
            (0, jnp.logical_and(low_x, blk3 > 0)),
            (2, high_y),
            (3, jnp.logical_and(high_y, grp3 < GRP - 1)),
            (3, low_y),
            (2, jnp.logical_and(low_y, grp3 > 0)),
            (4, lane3 >= 4),
            (5, lane3 < 124),
        )
        for n, (k, used) in enumerate(uses):
            moved = list(shifts_3(ws[k]))[n]
            f3[n] = jnp.where(used, rc * moved, 0.0)
        total = None
        for k in range(6):
            coarse = octet(ws[k]) * (1.0 / 32.0)
            f4[k] = coarse
            total = coarse if total is None else total + coarse
        rc = OMEGA / total
        rc4[...] = rc
        edge = (blk3 == 0, blk3 == BLK - 1, grp3 == 0, grp3 == GRP - 1, lane3 < 8, lane3 >= 120)
        for k in range(6):
            moved = list(shifts_4(f4[k]))[k]
            f4[k] = jnp.where(edge[k], 0.0, rc * moved)

    def sweep_3(v, big):
        out = KEEP * v + big
        for k, moved in enumerate(shifts_3(v)):
            out += f3[k] * moved
        return out

    def sweep_4(v, big):
        out = KEEP * v + big
        for k, moved in enumerate(shifts_4(v)):
            out += f4[k] * moved
        return out

    def coarse_levels(source):
        big = rc3[...] * source
        u = sweep_3(big, big)
        left = (sweep_3(u, big) - u) * cr3[...]
        big_4 = rc4[...] * (octet(left) * 0.125)
        v = lax.fori_loop(0, 7, lambda n, v: sweep_4(v, big_4), big_4, unroll=True)
        u = u + v
        u = sweep_3(u, big)
        return sweep_3(u, big)

    for c in range(CYCLES):
        arrived(g0_halo[c])

        def source_0(p, n):
            here = pl.ds(p, n)
            mask = mask0(p, n)
            for part in range(2):
                big0[part, here] = jnp.where(mask, g0[c, part, here], 0.0)

        planes(2, 22, 20, source_0)

        def down_0(p, n):
            here = pl.ds(p, n)
            a0[0, here], a0[1, here] = sweep_0(big0, p, n)

        planes(3, 21, 18, down_0)

        def restrict_0(p, n):
            here = pl.ds(p, n)
            e, o = sweep_0(a0, p, n)
            left = (e - a0[0, here]) * cr0[0, here] + (o - a0[1, here]) * cr0[1, here]
            m = n // 2
            tmp[0:m] = pairs(left)
            rows = tmp[0:m, pl.ds(4, 8, stride=2), :] + tmp[0:m, pl.ds(5, 8, stride=2), :]
            here = pl.ds((p // 2) - 2, m)
            there = pl.ds((p // 2) + 4, m)
            g1[c, there, 8:16, :] = rc1[here] * (rows * 0.125)

        planes(4, 20, 16, restrict_0)
        start(g1_halo[c])
        for part in range(2):
            x0[c, part, 4:20, 4:20, :] = a0[part, 4:20, 4:20, :]
        start(x0_halo[c])

        if c == 0:
            start(w2_halo)
            wait_for(w3.at[:, pl.ds(0, GRP - 1), pl.ds(0, 1), :], all_recv.at[0])
            block = w3.at[:, b]
            spread(block, block, [(dx, 0) for dx in range(1, BLK)], 1)
            start(w0_rest)
            arrived(w1_halo)
            planes(1, 19, 6, lambda p, n: fold_c(w1, f1, cr1, p, n, 1, mask1(p, n)))
        arrived(g1_halo[c])
        big1[...] = jnp.where(mask1(0, 20), g1[c], 0.0)
        a1[1:19] = sweep_c(big1, big1, f1, 1, 18, 1)
        left = (sweep_c(a1, big1, f1, 2, 16, 1) - a1[2:18]) * cr1[2:18]
        tmp[0:8] = pairs(left)
        rows = tmp[0:8, pl.ds(4, 8, stride=2), :] + tmp[0:8, pl.ds(5, 8, stride=2), :]
        g2[2:10, 2:10, :] = (rows + lane_swap(rows, 1)) * 0.125
        if c == 0:
            arrived(w2_halo)
            rc2[1:11] = fold_c(w2, f2, cr2, 1, 10, 2, mask2(1, 10))
        big2[2:10] = rc2[2:10] * g2[2:10]
        a2[3:9] = sweep_c(big2, big2, f2, 3, 6, 2)
        left = (sweep_c(a2, big2, f2, 4, 4, 2) - a2[4:8]) * cr2[4:8]
        left = pairs(left)
        tmp[0:2, 0:16, :] = (left + lane_swap(left, 2)) * 0.125
        cells = []
        for xl in range(2):
            for yl in range(2):
                cells.append(tmp[xl, pl.ds(4 + 2 * yl, 1), :] + tmp[xl, pl.ds(5 + 2 * yl, 1), :])
        g3row[c] = pack_quads(cells)
        spread_all(c)
        x2[c, 0, 4:8, 4:8, :] = big2[4:8, 4:8, :]
        x2[c, 1, 4:8, 4:8, :] = a2[4:8, 4:8, :]
        start(x2_halo[c])
        if c == 0:
            wait_for(w3.at[:, pl.ds(0, BLK - 1)], all_recv.at[1])
            fold_coarse()
            arrived(w0_rest)
            merge_0()
            planes(2, 22, 5, fold_0)
        wait_for(g3.at[c], all_recv.at[2 + c])
        c3[1:17] = coarse_levels(g3[c])

        near = c3[pl.ds(b, 3)]
        quads = lane_index((3, 8, 128)) & 3
        for xl in range(2):
            for yl in range(2):
                own = jnp.where(quads == 2 * xl + yl, near, 0.0)
                own = own + lane_swap(own, 1)
                own = own + lane_swap(own, 2)
                for dy in range(2):
                    t3[:, xl, pl.ds(8 + 2 * yl + dy, 8, stride=4), :] = own
        arrived(x2_halo[c])
        inside_2 = mask2(0, 12)
        big2[...] = jnp.where(inside_2, x2[c, 0], 0.0)
        add = doubled(t3[:, :, pl.ds(4 + 4 * g, 16), :].reshape(6, 16, 128))
        b2[...] = jnp.where(inside_2, x2[c, 1] + add, 0.0)
        a2[1:11] = sweep_c(b2, big2, f2, 1, 10, 2)
        t2[...] = sweep_c(a2, big2, f2, 2, 8, 2)
        rows = t2[:, 2:10, :]
        t1[:, pl.ds(4, 8, stride=2), :] = rows
        t1[:, pl.ds(5, 8, stride=2), :] = rows

        b1[2:18] = jnp.where(mask1(2, 16), a1[2:18] + doubled(t1[...]), 0.0)
        a1[3:17] = sweep_c(b1, big1, f1, 3, 14, 1)
        tmp[...] = sweep_c(a1, big1, f1, 4, 12, 1)
        rows = tmp[:, 6:18, :]
        s0[:, pl.ds(0, 12, stride=2), :] = rows
        s0[:, pl.ds(1, 12, stride=2), :] = rows

        arrived(x0_halo[c])

        def correct_0(p, n):
            here = pl.ds(p, n)
            add = doubled(s0[pl.ds((p // 2), n // 2)])
            mask = mask0(p, n)
            for part in range(2):
                b0[part, here] = jnp.where(mask, x0[c, part, here] + add, 0.0)

        planes(0, 24, 24, correct_0)

        def up_0a(p, n):
            here = pl.ds(p, n)
            a0[0, here], a0[1, here] = sweep_0(b0, p, n)

        planes(2, 22, 20, up_0a)

        def up_0b(p, n):
            here = pl.ds(p, n)
            b0[0, here], b0[1, here] = sweep_0(a0, p, n)

        planes(3, 21, 18, up_0b)

        def update(p, n):
            here, out = pl.ds(p, n), pl.ds(p - 4, n)
            swept = sweep_0(b0, p, n)
            for part in range(2):
                lanes = pl.ds(128 * part, 128)
                u = b0[part, here]
                change = swept[part] - u
                if c + 1 < CYCLES:
                    g0[c + 1, part, here, 4:20, :] = change[:, 4:20, :]
                else:
                    res_ref[out, :, lanes] = (change * cr0[part, here])[:, 4:20, :]
                u = u[:, 4:20, :]
                sol_ref[out, :, lanes] = u if c == 0 else sol_ref[out, :, lanes] + u

        planes(4, 20, 16, update)
        if c + 1 < CYCLES:
            start(g0_halo[c + 1])

    for one in batches:
        departed(one)
    wait_for(w3.at[:, pl.ds(0, GRP - 1), pl.ds(0, 1), :], all_send.at[0])
    wait_for(w3.at[:, pl.ds(0, BLK - 1)], all_send.at[1])
    for c in cycles:
        wait_for(dummy1, all_send.at[2 + c])


def join_kernel(sol_in, res_in, sol_out, res_out, whole, store_sem):
    stores = [pltpu.make_async_copy(whole.at[n], ref, store_sem.at[n]) for n, ref in enumerate((sol_out, res_out))]
    zi = lax.broadcasted_iota(jnp.int32, (256, 256), 1)
    ci = lax.broadcasted_iota(jnp.int32, (256, 256), 0)
    parted = jnp.where(ci < 128, 2 * ci, 2 * ci - 255)
    joined = jnp.where(zi == parted, 1.0, 0.0).astype(jnp.bfloat16)
    for n, ref in enumerate((sol_in, res_in)):
        whole[n] = split_dot(ref[...].reshape(256, 256), joined).reshape(16, 16, 256)
        stores[n].start()
    for copy in stores:
        copy.wait()


def body(right_side, weights):
    vmem = pl.BlockSpec(memory_space=pltpu.VMEM)
    field = jax.ShapeDtypeStruct((16, 16, 256), F32)
    f0 = (24, 24, 128)
    f1 = (20, 24, 128)
    f2 = (12, 16, 128)
    f3 = (BLK, GRP, 128)

    def buf(*shape):
        return pltpu.VMEM(shape, F32)

    parted = pl.pallas_call(
        kernel,
        out_shape=(buf(16, 16, 256), buf(16, 16, 256)),
        in_specs=[pl.BlockSpec(memory_space=pl.ANY)] * 2,
        out_specs=(vmem, vmem),
        scratch_shapes=[
            buf(7, 16, 16, 256),
            buf(12, *f0), buf(12, *f0), buf(2, *f0), buf(2, 2, *f0), buf(2, *f0),
            buf(2, *f0), buf(2, *f0), buf(2, 2, *f0), buf(12, 24, 128),
            buf(6, *f1), buf(6, *f1), buf(8, 8, 128), buf(*f1), buf(2, *f1), buf(*f1), buf(*f1), buf(*f1), buf(8, 24, 128),
            buf(6, *f2), buf(6, *f2), buf(*f2), buf(*f2), buf(*f2), buf(2, 2, *f2), buf(*f2), buf(*f2), buf(*f2),
            buf(8, 16, 128),
            buf(6, *f3), buf(10, *f3), buf(*f3), buf(*f3), buf(2, 1, 128), buf(2, *f3),
            buf(18, 8, 128), buf(3, 2, 48, 128),
            buf(6, *f3), buf(*f3), buf(12, 24, 128), buf(2048, 128), buf(127, 1, 128), buf(12, *f0),
            pltpu.SemaphoreType.DMA((7,)),
            pltpu.SemaphoreType.DMA((12,)),
            pltpu.SemaphoreType.DMA((12,)),
            pltpu.SemaphoreType.DMA((4,)),
            pltpu.SemaphoreType.DMA((4,)),
        ],
        compiler_params=pltpu.CompilerParams(
            collective_id=0, has_side_effects=True, vmem_limit_bytes=56 * 1024 * 1024
        ),
    )(right_side, weights)
    return pl.pallas_call(
        join_kernel,
        out_shape=(field, field),
        in_specs=[vmem, vmem],
        out_specs=[pl.BlockSpec(memory_space=pltpu.HBM)] * 2,
        scratch_shapes=[
            buf(2, 16, 16, 256), pltpu.SemaphoreType.DMA((2,)),
        ],
        compiler_params=pltpu.CompilerParams(vmem_limit_bytes=48 * 1024 * 1024),
    )(*parted)


def solution(mesh):
    return jax.shard_map(
        body,
        mesh=mesh,
        in_specs=(P("blk", "grp", None), P(None, "blk", "grp", None)),
        out_specs=(P("blk", "grp", None), P("blk", "grp", None)),
        check_vma=False,
    )
```

```python
import functools

import jax
import jax.numpy as jnp
from jax import lax
from jax.experimental import pallas as pl
from jax.experimental.pallas import tpu as pltpu
from jax.sharding import PartitionSpec as P

MESH = pl.DeviceIdType.MESH
F32 = jnp.float32
BLK, GRP = 16, 8
OMEGA = 0.7
KEEP = 1.0 - OMEGA
FACES = ((1, 0), (-1, 0), (0, 1), (0, -1))
CORNERS = ((1, 1), (1, -1), (-1, 1), (-1, -1))


def distance(offset):
    dx, dy = offset
    x, y, z = dx % 4, dy // 2, dx // 4
    return min(x, 4 - x) + min(y, 4 - y) + min(z, 4 - z)


EVERYONE = sorted(((dx, dy) for dx in range(BLK) for dy in range(GRP) if dx or dy), key=distance, reverse=True)
CYCLES = 2


def lane_roll(v, n):
    return pltpu.roll(v, n % 128, v.ndim - 1)


def row_roll(v, n):
    axis = v.ndim - 2
    return pltpu.roll(v, n % v.shape[axis], axis)


def lane_index(shape):
    return lax.broadcasted_iota(jnp.int32, shape, len(shape) - 1)


def lane_swap(v, n):
    even = (lane_index(v.shape[-2:]) & n) == 0
    even = jnp.broadcast_to(even, v.shape)
    return jnp.where(even, lane_roll(v, -n), lane_roll(v, n))


def split_dot(x, matrix):
    high = x.astype(jnp.bfloat16)
    rest = x - high.astype(F32)
    middle = rest.astype(jnp.bfloat16)
    low = (rest - middle.astype(F32)).astype(jnp.bfloat16)
    dot = functools.partial(jnp.dot, preferred_element_type=F32)
    return (dot(low, matrix) + dot(middle, matrix)) + dot(high, matrix)


def piece(delta, size, start, first, count):
    if delta == 1:
        return pl.ds(start + size + 1 - first - count, count), pl.ds(start + 1 - first - count, count)
    if delta == -1:
        return pl.ds(start + first - 1, count), pl.ds(start + size + first - 1, count)
    return pl.ds(start, size), pl.ds(start, size)


def kernel(
    rhs_ref, w_ref, sol_ref, res_ref,
    raw, w0, f0, cr0, g0, big0, a0, b0, x0, s0,
    w1, f1, rc1, cr1, g1, big1, a1, b1, t1,
    w2, f2, rc2, cr2, g2, x2, big2, a2, b2, t2,
    w3, f3, rc3, cr3, g3row, g3, c3, t3,
    f4, rc4, tmp, dummy, dummy1, w0x,
    load_sem, send_sem, recv_sem, all_send, all_recv,
):
    b = lax.axis_index("blk")
    g = lax.axis_index("grp")

    loads = [pltpu.make_async_copy(w_ref.at[k], raw.at[k], load_sem.at[k]) for k in range(6)]
    loads.append(pltpu.make_async_copy(rhs_ref, raw.at[6], load_sem.at[6]))
    for copy in loads:
        copy.start()

    def device(dx, dy):
        return (lax.rem(b + dx + BLK, BLK), lax.rem(g + dy + GRP, GRP))

    barrier = pltpu.get_barrier_semaphore()

    def greet(dx, dy):
        pl.semaphore_signal(barrier, inc=1, device_id=device(dx, dy), device_id_type=MESH)

    def greet_block(dx, carry):
        for dy in range(GRP):
            greet(dx, dy)
        return carry

    for dy in range(1, GRP):
        greet(0, dy)
    lax.fori_loop(1, BLK, greet_block, 0)

    def loop(begin, end, step):
        def one(index, carry):
            step(index)
            return carry

        lax.fori_loop(begin, end, one, 0)

    def patch(view, lead, fields, level, dx, dy, layers_x, layers_y, into=None):
        into = view if into is None else into
        size, start_x, start_y = level
        sx, tx = piece(dx, size, start_x, *layers_x)
        sy, ty = piece(dy, size, start_y, *layers_y)
        rows = fields * (layers_x[1] if dx else size) * (layers_y[1] if dy else size)
        return view.at[lead + (sx, sy)], into.at[lead + (tx, ty)], device(dx, dy), rows

    def faces(view, lead, fields, level, layers, into=None):
        return [patch(view, lead, fields, level, dx, dy, layers, layers, into) for dx, dy in FACES]

    def corners(view, lead, fields, level, layers_x, layers_y, into=None):
        return [
            patch(view, lead, fields, level, dx, dy, layers_x, layers_y, into) for dx, dy in CORNERS
        ]

    def inward(view, each, level, layer, into=None):
        return [
            patch(view, (pl.ds(k * each, each),), each, level, dx, dy, (layer, 1), (layer, 1), into)
            for k, (dx, dy) in enumerate(FACES)
        ]

    batches = []

    def batch(parts):
        index = len(batches)
        copies = [
            pltpu.make_async_remote_copy(
                src_ref=src,
                dst_ref=dst,
                send_sem=send_sem.at[index],
                recv_sem=recv_sem.at[index],
                device_id=to,
                device_id_type=MESH,
            )
            for src, dst, to, _ in parts
        ]
        rows = sum(part[3] for part in parts)
        batches.append((copies, dummy.at[pl.ds(0, rows)], index))
        return batches[-1]

    def start(one):
        for copy in one[0]:
            copy.start()

    def arrived(one):
        pltpu.make_async_copy(one[1], one[1], recv_sem.at[one[2]]).wait()

    def departed(one):
        pltpu.make_async_copy(one[1], one[1], send_sem.at[one[2]]).wait()

    def spread(src, dst, offsets, slot):
        for dx, dy in offsets:
            pltpu.make_async_remote_copy(
                src_ref=src,
                dst_ref=dst,
                send_sem=all_send.at[slot],
                recv_sem=all_recv.at[slot],
                device_id=device(dx, dy),
                device_id_type=MESH,
            ).start()

    def spread_all(c):
        row, mine = g3row.at[c], g3.at[c, b, pl.ds(g, 1), :]
        pltpu.make_async_copy(row, mine, all_recv.at[2 + c]).start()
        spread(row, mine, EVERYONE, 2 + c)

    def wait_for(ref, sem):
        pltpu.make_async_copy(ref, ref, sem).wait()

    def inside(rows, size, start_x, start_y):
        def mask(p, n):
            shape = (n, rows, 128)
            x = lax.broadcasted_iota(jnp.int32, shape, 0) + (b * size + p - start_x)
            y = lax.broadcasted_iota(jnp.int32, shape, 1) + (g * size - start_y)
            ok_x = jnp.logical_and(x >= 0, x < BLK * size)
            ok_y = jnp.logical_and(y >= 0, y < GRP * size)
            return jnp.logical_and(ok_x, ok_y)

        return mask

    def planes(begin, end, size, step):
        count = (end - begin) // size
        if count == 1:
            step(begin, size)
        elif count > 1:
            loop(0, count, lambda i: step(begin + i * size, size))
        if end - begin > count * size:
            step(begin + count * size, end - begin - count * size)

    def pairs(v):
        both = v.reshape((v.shape[0] // 2, 2) + v.shape[1:])
        return both[:, 0] + both[:, 1]

    def doubled(v):
        wide = jnp.broadcast_to(v[:, None], (v.shape[0], 2) + v.shape[1:])
        return wide.reshape((2 * v.shape[0],) + v.shape[1:])

    zi = lax.broadcasted_iota(jnp.int32, (256, 256), 0)
    ci = lax.broadcasted_iota(jnp.int32, (256, 256), 1)
    parted = jnp.where(ci < 128, 2 * ci, 2 * ci - 255)
    split = jnp.where(zi == parted, 1.0, 0.0).astype(jnp.bfloat16)

    def part_weights(i):
        first = 3 * i
        for k in range(3):
            pltpu.make_async_copy(w_ref.at[first + k], raw.at[first + k], load_sem.at[first + k]).wait()
        both = split_dot(raw[pl.ds(first, 3)].reshape(768, 256), split).reshape(3, 16, 16, 256)
        for k in range(3):
            for part in range(2):
                w0[2 * (first + k) + part, 4:20, 4:20, :] = both[k, :, :, 128 * part : 128 * part + 128]

    loop(0, 2, part_weights)

    pl.semaphore_wait(barrier, BLK * GRP - 1)

    every = slice(None)
    level_0, level_1, level_2 = (16, 4, 4), (8, 6, 8), (4, 4, 4)

    def halo(view, lead, fields, level, layers, corner):
        return corners(view, lead, fields, level, (1, corner), (1, corner)) + faces(
            view, lead, fields, level, (1, layers)
        )

    cycles = range(CYCLES)
    g0_halo = [batch(halo(g0, (c, every), 2, level_0, 2, 1)) for c in cycles]
    g1_halo = [batch(halo(g1, (c,), 1, level_1, 6, 5)) for c in cycles]
    x0_halo = [batch(halo(x0, (c, every), 2, level_0, 3, 2)) for c in cycles]
    x2_halo = [batch(halo(x2, (c, every), 2, level_2, 4, 4)) for c in cycles]
    w0_halo = batch(halo(w0, (every,), 12, level_0, 1, 1) + inward(w0, 2, level_0, 2))
    w0_rest = batch(
        faces(w0, (every,), 12, level_0, (2, 1), w0x)
        + corners(w0, (every,), 12, level_0, (1, 2), (1, 2), w0x)
        + inward(w0, 2, level_0, 3, w0x)
    )
    w1_halo = batch(
        halo(w1, (every,), 6, level_1, 5, 3)
        + inward(w1, 1, level_1, 6)
        + corners(w1, (every,), 6, level_1, (4, 2), (1, 2))
        + corners(w1, (every,), 6, level_1, (1, 2), (4, 2))
    )
    w2_halo = batch(halo(w2, (every,), 6, level_2, 3, 4) + inward(w2, 1, level_2, 4))

    start(w0_halo)
    loads[6].wait()
    both = split_dot(raw[6].reshape(256, 256), split)
    for part in range(2):
        total = w0[part, 4:20, 4:20, :]
        for k in range(1, 6):
            total = total + w0[2 * k + part, 4:20, 4:20, :]
        source = both[:, 128 * part : 128 * part + 128].reshape(16, 16, 128)
        g0[0, part, 4:20, 4:20, :] = (OMEGA / total) * source
    start(g0_halo[0])

    def weights_1(k):
        total = None
        for part in range(2):
            for dy in range(2):
                term = pairs(w0[2 * k + part, 4:20, pl.ds(4 + dy, 8, stride=2), :])
                total = term if total is None else total + term
        w1[k, 6:14, 8:16, :] = total * (1.0 / 32.0)

    loop(0, 6, weights_1)
    start(w1_halo)
    total = w1[0, 6:14, 8:16, :]
    for k in range(1, 6):
        total = total + w1[k, 6:14, 8:16, :]
    rc1[...] = OMEGA / total
    for k in range(6):
        total = None
        for dy in range(2):
            term = pairs(w1[k, 6:14, pl.ds(8 + dy, 4, stride=2), :])
            total = term if total is None else total + term
        w2[k, 4:8, 4:8, :] = (total + lane_swap(total, 1)) * (1.0 / 32.0)

    quad = lane_index((1, 128)) & 3

    def pack_quads(cells):
        out = cells[3]
        for n in range(3):
            out = jnp.where(quad == n, cells[n], out)
        return out

    for k in range(6):
        total = pairs(w2[k, 4:8, 4:8, :])
        total = (total + lane_swap(total, 2)) * (1.0 / 32.0)
        cells = []
        for xl in range(2):
            for yl in range(2):
                cells.append(total[xl, 2 * yl : 2 * yl + 1] + total[xl, 2 * yl + 1 : 2 * yl + 2])
        w3[k, b, pl.ds(g, 1), :] = pack_quads(cells)
    mine = w3.at[:, b, pl.ds(g, 1), :]
    spread(mine, mine, [(0, dy) for dy in range(1, GRP)], 0)

    mask0 = inside(24, 16, 4, 4)
    mask1 = inside(24, 8, 6, 8)
    mask2 = inside(16, 4, 4, 4)

    def relaxed(total, mask):
        return jnp.where(mask, OMEGA / total, 0.0)

    arrived(w0_halo)

    def fold_0(p, n):
        here, low, high = pl.ds(p, n), pl.ds(p - 1, n), pl.ds(p + 1, n)
        mask = mask0(p, n)
        lanes = lane_index((n, 24, 128))
        rc = []
        for part in range(2):
            total = w0[part, here]
            for k in range(1, 6):
                total = total + w0[2 * k + part, here]
            rc.append(relaxed(total, mask))
            cr0[part, here] = total * (1.0 / OMEGA)
            f0[0 + part, here] = rc[part] * w0[0 + part, low]
            f0[2 + part, here] = rc[part] * w0[2 + part, high]
            f0[4 + part, here] = rc[part] * row_roll(w0[4 + part, here], 1)
            f0[6 + part, here] = rc[part] * row_roll(w0[6 + part, here], -1)
        f0[8, here] = rc[0] * jnp.where(lanes == 0, 0.0, lane_roll(w0[9, here], 1))
        f0[9, here] = rc[1] * w0[8, here]
        f0[10, here] = rc[0] * w0[11, here]
        f0[11, here] = rc[1] * jnp.where(lanes == 127, 0.0, lane_roll(w0[10, here], -1))

    planes(3, 21, 9, fold_0)

    def merge_0():
        for x in (2, 21):
            w0[:, x, 4:20, :] = w0x[:, x, 4:20, :]
        for y in (2, 21):
            w0[:, 4:20, y : y + 1, :] = w0x[:, 4:20, y : y + 1, :]
        for x in (2, 20):
            for y in (2, 20):
                w0[:, x : x + 2, y : y + 2, :] = w0x[:, x : x + 2, y : y + 2, :]
        w0[0:2, 1, 4:20, :] = w0x[0:2, 1, 4:20, :]
        w0[2:4, 22, 4:20, :] = w0x[2:4, 22, 4:20, :]
        w0[4:6, 4:20, 1:2, :] = w0x[4:6, 4:20, 1:2, :]
        w0[6:8, 4:20, 22:23, :] = w0x[6:8, 4:20, 22:23, :]

    def sweep_0(u, p, n):
        here, low, high = pl.ds(p, n), pl.ds(p - 1, n), pl.ds(p + 1, n)
        e, o = u[0, here], u[1, here]
        out_e = KEEP * e + big0[0, here]
        out_o = KEEP * o + big0[1, here]
        out_e += f0[0, here] * u[0, low]
        out_o += f0[1, here] * u[1, low]
        out_e += f0[2, here] * u[0, high]
        out_o += f0[3, here] * u[1, high]
        out_e += f0[4, here] * row_roll(e, 1)
        out_o += f0[5, here] * row_roll(o, 1)
        out_e += f0[6, here] * row_roll(e, -1)
        out_o += f0[7, here] * row_roll(o, -1)
        out_e += f0[8, here] * lane_roll(o, 1)
        out_o += f0[9, here] * e
        out_e += f0[10, here] * o
        out_o += f0[11, here] * lane_roll(e, -1)
        return out_e, out_o

    def sweep_c(u, big, f, p, n, step):
        here = pl.ds(p, n)
        v = u[here]
        out = KEEP * v + big[here]
        out += f[0, here] * u[pl.ds(p - 1, n)]
        out += f[1, here] * u[pl.ds(p + 1, n)]
        out += f[2, here] * row_roll(v, 1)
        out += f[3, here] * row_roll(v, -1)
        out += f[4, here] * lane_roll(v, step)
        out += f[5, here] * lane_roll(v, -step)
        return out

    def fold_c(w, f, cr, p, n, step, mask):
        here = pl.ds(p, n)
        total = w[0, here]
        for k in range(1, 6):
            total = total + w[k, here]
        r = relaxed(total, mask)
        cr[here] = total * (1.0 / OMEGA)
        lanes = lane_index(r.shape)
        f[0, here] = r * w[0, pl.ds(p - 1, n)]
        f[1, here] = r * w[1, pl.ds(p + 1, n)]
        f[2, here] = r * row_roll(w[2, here], 1)
        f[3, here] = r * row_roll(w[3, here], -1)
        f[4, here] = r * jnp.where(lanes < step, 0.0, lane_roll(w[4, here], step))
        f[5, here] = r * jnp.where(lanes >= 128 - step, 0.0, lane_roll(w[5, here], -step))
        return r

    shape3 = (BLK, GRP, 128)

    def before(v):
        return jnp.concatenate([v[BLK - 1 :], v[: BLK - 1]], axis=0)

    def after(v):
        return jnp.concatenate([v[1:], v[:1]], axis=0)

    lane3 = lane_index(shape3)
    blk3 = lax.broadcasted_iota(jnp.int32, shape3, 0)
    grp3 = lax.broadcasted_iota(jnp.int32, shape3, 1)
    low_x = (lane3 & 2) == 0
    low_y = (lane3 & 1) == 0

    def shifts_3(v):
        moved = lane_roll(v, 2)
        yield moved
        yield after(moved)
        moved = lane_roll(v, -2)
        yield moved
        yield before(moved)
        moved = lane_roll(v, 1)
        yield moved
        yield row_roll(moved, -1)
        moved = lane_roll(v, -1)
        yield moved
        yield row_roll(moved, 1)
        yield lane_roll(v, 4)
        yield lane_roll(v, -4)

    def shifts_4(v):
        yield before(v)
        yield after(v)
        yield row_roll(v, 1)
        yield row_roll(v, -1)
        yield lane_roll(v, 8)
        yield lane_roll(v, -8)

    def octet(v):
        v = v + lane_swap(v, 1)
        v = v + lane_swap(v, 2)
        return v + lane_swap(v, 4)

    def fold_coarse():
        ws = [w3[k] for k in range(6)]
        total = ws[0] + ws[1] + ws[2] + ws[3] + ws[4] + ws[5]
        rc = OMEGA / total
        rc3[...] = rc
        cr3[...] = total * (1.0 / OMEGA)
        high_x, high_y = jnp.logical_not(low_x), jnp.logical_not(low_y)
        uses = (
            (0, high_x),
            (1, jnp.logical_and(high_x, blk3 < BLK - 1)),
            (1, low_x),
            (0, jnp.logical_and(low_x, blk3 > 0)),
            (2, high_y),
            (3, jnp.logical_and(high_y, grp3 < GRP - 1)),
            (3, low_y),
            (2, jnp.logical_and(low_y, grp3 > 0)),
            (4, lane3 >= 4),
            (5, lane3 < 124),
        )
        for n, (k, used) in enumerate(uses):
            moved = list(shifts_3(ws[k]))[n]
            f3[n] = jnp.where(used, rc * moved, 0.0)
        total = None
        for k in range(6):
            coarse = octet(ws[k]) * (1.0 / 32.0)
            f4[k] = coarse
            total = coarse if total is None else total + coarse
        rc = OMEGA / total
        rc4[...] = rc
        edge = (blk3 == 0, blk3 == BLK - 1, grp3 == 0, grp3 == GRP - 1, lane3 < 8, lane3 >= 120)
        for k in range(6):
            moved = list(shifts_4(f4[k]))[k]
            f4[k] = jnp.where(edge[k], 0.0, rc * moved)

    def sweep_3(v, big):
        out = KEEP * v + big
        for k, moved in enumerate(shifts_3(v)):
            out += f3[k] * moved
        return out

    def sweep_4(v, big):
        out = KEEP * v + big
        for k, moved in enumerate(shifts_4(v)):
            out += f4[k] * moved
        return out

    def coarse_levels(source):
        big = rc3[...] * source
        u = sweep_3(big, big)
        left = (sweep_3(u, big) - u) * cr3[...]
        big_4 = rc4[...] * (octet(left) * 0.125)
        v = lax.fori_loop(0, 7, lambda n, v: sweep_4(v, big_4), big_4, unroll=True)
        u = u + v
        u = sweep_3(u, big)
        return sweep_3(u, big)

    for c in range(CYCLES):
        arrived(g0_halo[c])

        def source_0(p, n):
            here = pl.ds(p, n)
            mask = mask0(p, n)
            for part in range(2):
                big0[part, here] = jnp.where(mask, g0[c, part, here], 0.0)

        planes(2, 22, 20, source_0)

        def down_0(p, n):
            here = pl.ds(p, n)
            a0[0, here], a0[1, here] = sweep_0(big0, p, n)

        planes(3, 21, 18, down_0)

        def restrict_0(p, n):
            here = pl.ds(p, n)
            e, o = sweep_0(a0, p, n)
            left = (e - a0[0, here]) * cr0[0, here] + (o - a0[1, here]) * cr0[1, here]
            m = n // 2
            tmp[0:m] = pairs(left)
            rows = tmp[0:m, pl.ds(4, 8, stride=2), :] + tmp[0:m, pl.ds(5, 8, stride=2), :]
            here = pl.ds((p // 2) - 2, m)
            there = pl.ds((p // 2) + 4, m)
            g1[c, there, 8:16, :] = rc1[here] * (rows * 0.125)

        planes(4, 20, 16, restrict_0)
        start(g1_halo[c])
        for part in range(2):
            x0[c, part, 4:20, 4:20, :] = a0[part, 4:20, 4:20, :]
        start(x0_halo[c])

        if c == 0:
            start(w2_halo)
            wait_for(w3.at[:, pl.ds(0, GRP - 1), pl.ds(0, 1), :], all_recv.at[0])
            block = w3.at[:, b]
            spread(block, block, [(dx, 0) for dx in range(1, BLK)], 1)
            arrived(w1_halo)
            planes(1, 19, 6, lambda p, n: fold_c(w1, f1, cr1, p, n, 1, mask1(p, n)))
        arrived(g1_halo[c])
        if c == 0:
            start(w0_rest)
        big1[...] = jnp.where(mask1(0, 20), g1[c], 0.0)
        a1[1:19] = sweep_c(big1, big1, f1, 1, 18, 1)
        left = (sweep_c(a1, big1, f1, 2, 16, 1) - a1[2:18]) * cr1[2:18]
        tmp[0:8] = pairs(left)
        rows = tmp[0:8, pl.ds(4, 8, stride=2), :] + tmp[0:8, pl.ds(5, 8, stride=2), :]
        g2[2:10, 2:10, :] = (rows + lane_swap(rows, 1)) * 0.125
        if c == 0:
            arrived(w2_halo)
            rc2[1:11] = fold_c(w2, f2, cr2, 1, 10, 2, mask2(1, 10))
        big2[2:10] = rc2[2:10] * g2[2:10]
        a2[3:9] = sweep_c(big2, big2, f2, 3, 6, 2)
        left = (sweep_c(a2, big2, f2, 4, 4, 2) - a2[4:8]) * cr2[4:8]
        left = pairs(left)
        tmp[0:2, 0:16, :] = (left + lane_swap(left, 2)) * 0.125
        cells = []
        for xl in range(2):
            for yl in range(2):
                cells.append(tmp[xl, pl.ds(4 + 2 * yl, 1), :] + tmp[xl, pl.ds(5 + 2 * yl, 1), :])
        g3row[c] = pack_quads(cells)
        spread_all(c)
        x2[c, 0, 4:8, 4:8, :] = big2[4:8, 4:8, :]
        x2[c, 1, 4:8, 4:8, :] = a2[4:8, 4:8, :]
        start(x2_halo[c])
        if c == 0:
            wait_for(w3.at[:, pl.ds(0, BLK - 1)], all_recv.at[1])
            fold_coarse()
            arrived(w0_rest)
            merge_0()
            planes(2, 22, 5, fold_0)
        wait_for(g3.at[c], all_recv.at[2 + c])
        c3[1:17] = coarse_levels(g3[c])

        near = c3[pl.ds(b, 3)]
        quads = lane_index((3, 8, 128)) & 3
        for xl in range(2):
            for yl in range(2):
                own = jnp.where(quads == 2 * xl + yl, near, 0.0)
                own = own + lane_swap(own, 1)
                own = own + lane_swap(own, 2)
                for dy in range(2):
                    t3[:, xl, pl.ds(8 + 2 * yl + dy, 8, stride=4), :] = own
        arrived(x2_halo[c])
        inside_2 = mask2(0, 12)
        big2[...] = jnp.where(inside_2, x2[c, 0], 0.0)
        add = doubled(t3[:, :, pl.ds(4 + 4 * g, 16), :].reshape(6, 16, 128))
        b2[...] = jnp.where(inside_2, x2[c, 1] + add, 0.0)
        a2[1:11] = sweep_c(b2, big2, f2, 1, 10, 2)
        t2[...] = sweep_c(a2, big2, f2, 2, 8, 2)
        rows = t2[:, 2:10, :]
        t1[:, pl.ds(4, 8, stride=2), :] = rows
        t1[:, pl.ds(5, 8, stride=2), :] = rows

        b1[2:18] = jnp.where(mask1(2, 16), a1[2:18] + doubled(t1[...]), 0.0)
        a1[3:17] = sweep_c(b1, big1, f1, 3, 14, 1)
        tmp[...] = sweep_c(a1, big1, f1, 4, 12, 1)
        rows = tmp[:, 6:18, :]
        s0[:, pl.ds(0, 12, stride=2), :] = rows
        s0[:, pl.ds(1, 12, stride=2), :] = rows

        arrived(x0_halo[c])

        def correct_0(p, n):
            here = pl.ds(p, n)
            add = doubled(s0[pl.ds((p // 2), n // 2)])
            mask = mask0(p, n)
            for part in range(2):
                b0[part, here] = jnp.where(mask, x0[c, part, here] + add, 0.0)

        planes(0, 24, 24, correct_0)

        def up_0a(p, n):
            here = pl.ds(p, n)
            a0[0, here], a0[1, here] = sweep_0(b0, p, n)

        planes(2, 22, 20, up_0a)

        def up_0b(p, n):
            here = pl.ds(p, n)
            b0[0, here], b0[1, here] = sweep_0(a0, p, n)

        planes(3, 21, 18, up_0b)

        def update(p, n):
            here, out = pl.ds(p, n), pl.ds(p - 4, n)
            swept = sweep_0(b0, p, n)
            for part in range(2):
                lanes = pl.ds(128 * part, 128)
                u = b0[part, here]
                change = swept[part] - u
                if c + 1 < CYCLES:
                    g0[c + 1, part, here, 4:20, :] = change[:, 4:20, :]
                else:
                    res_ref[out, :, lanes] = (change * cr0[part, here])[:, 4:20, :]
                u = u[:, 4:20, :]
                sol_ref[out, :, lanes] = u if c == 0 else sol_ref[out, :, lanes] + u

        planes(4, 20, 16, update)
        if c + 1 < CYCLES:
            start(g0_halo[c + 1])

    for one in batches:
        departed(one)
    wait_for(w3.at[:, pl.ds(0, GRP - 1), pl.ds(0, 1), :], all_send.at[0])
    wait_for(w3.at[:, pl.ds(0, BLK - 1)], all_send.at[1])
    for c in cycles:
        wait_for(dummy1, all_send.at[2 + c])


def join_kernel(sol_in, res_in, sol_out, res_out, whole, store_sem):
    stores = [pltpu.make_async_copy(whole.at[n], ref, store_sem.at[n]) for n, ref in enumerate((sol_out, res_out))]
    zi = lax.broadcasted_iota(jnp.int32, (256, 256), 1)
    ci = lax.broadcasted_iota(jnp.int32, (256, 256), 0)
    parted = jnp.where(ci < 128, 2 * ci, 2 * ci - 255)
    joined = jnp.where(zi == parted, 1.0, 0.0).astype(jnp.bfloat16)
    for n, ref in enumerate((sol_in, res_in)):
        whole[n] = split_dot(ref[...].reshape(256, 256), joined).reshape(16, 16, 256)
        stores[n].start()
    for copy in stores:
        copy.wait()


def body(right_side, weights):
    vmem = pl.BlockSpec(memory_space=pltpu.VMEM)
    field = jax.ShapeDtypeStruct((16, 16, 256), F32)
    f0 = (24, 24, 128)
    f1 = (20, 24, 128)
    f2 = (12, 16, 128)
    f3 = (BLK, GRP, 128)

    def buf(*shape):
        return pltpu.VMEM(shape, F32)

    parted = pl.pallas_call(
        kernel,
        out_shape=(buf(16, 16, 256), buf(16, 16, 256)),
        in_specs=[pl.BlockSpec(memory_space=pl.ANY)] * 2,
        out_specs=(vmem, vmem),
        scratch_shapes=[
            buf(7, 16, 16, 256),
            buf(12, *f0), buf(12, *f0), buf(2, *f0), buf(2, 2, *f0), buf(2, *f0),
            buf(2, *f0), buf(2, *f0), buf(2, 2, *f0), buf(12, 24, 128),
            buf(6, *f1), buf(6, *f1), buf(8, 8, 128), buf(*f1), buf(2, *f1), buf(*f1), buf(*f1), buf(*f1), buf(8, 24, 128),
            buf(6, *f2), buf(6, *f2), buf(*f2), buf(*f2), buf(*f2), buf(2, 2, *f2), buf(*f2), buf(*f2), buf(*f2),
            buf(8, 16, 128),
            buf(6, *f3), buf(10, *f3), buf(*f3), buf(*f3), buf(2, 1, 128), buf(2, *f3),
            buf(18, 8, 128), buf(3, 2, 48, 128),
            buf(6, *f3), buf(*f3), buf(12, 24, 128), buf(2048, 128), buf(127, 1, 128), buf(12, *f0),
            pltpu.SemaphoreType.DMA((7,)),
            pltpu.SemaphoreType.DMA((12,)),
            pltpu.SemaphoreType.DMA((12,)),
            pltpu.SemaphoreType.DMA((4,)),
            pltpu.SemaphoreType.DMA((4,)),
        ],
        compiler_params=pltpu.CompilerParams(
            collective_id=0, has_side_effects=True, vmem_limit_bytes=56 * 1024 * 1024
        ),
    )(right_side, weights)
    return pl.pallas_call(
        join_kernel,
        out_shape=(field, field),
        in_specs=[vmem, vmem],
        out_specs=[pl.BlockSpec(memory_space=pltpu.HBM)] * 2,
        scratch_shapes=[
            buf(2, 16, 16, 256), pltpu.SemaphoreType.DMA((2,)),
        ],
        compiler_params=pltpu.CompilerParams(vmem_limit_bytes=48 * 1024 * 1024),
    )(*parted)


def solution(mesh):
    return jax.shard_map(
        body,
        mesh=mesh,
        in_specs=(P("blk", "grp", None), P(None, "blk", "grp", None)),
        out_specs=(P("blk", "grp", None), P("blk", "grp", None)),
        check_vma=False,
    )
```
